32 devices in a mesh: dp: 8 (over z, core), et: 4 (over y, x).
Axes of the slice: x: 2, y: 2, z: 4, core: 2. Of those that a mesh axis runs over, the one named last changes fastest.
Arguments:
- pre_gate: bfloat16 [2048, 5376], P('dp', 'et'), may hold values from -6 to 6
- pre_up: bfloat16 [2048, 5376], P('dp', 'et'), may hold values from -6 to 6
- down_weight: bfloat16 [5376, 6144], P('et'), may hold values from -0.078125 to 0.078125
- row_token: int32 [2048], P('dp'), may hold values from 0 to 384, as said below
- block_count: int32 [8], P('dp'), may hold values from 1 to 2, as said below
- router_logits: float32 [3072, 16], P('dp'), as said below
- tokens_in: bfloat16 [3072, 6144], P('dp', 'et'), may hold values from -6 to 6
- out_grad: bfloat16 [3072, 6144], P('dp', 'et'), may hold values from -12 to 12
Outputs:
- combined: bfloat16 [3072, 6144], P('dp', 'et')
- grad_gate: bfloat16 [2048, 5376], P('dp', 'et')
- grad_up: bfloat16 [2048, 5376], P('dp', 'et')
- router_grad: float32 [16, 6144], P(None, 'et')
The draws below stay inside these ranges and needn't reach their ends.
Inputs may be any that keep to these rules, and one draw needn't show every extreme that they name: `row_token`: within the 256 slots of one index of dp, the first r slots hold distinct tokens below 384 and the other slots hold 384, with r between 64 and 256; r = 256 on at least one index of dp. `block_count`: the number of blocks of 128 slots that hold r's live slots, rounded up, on each index of dp. `router_logits`: finite router scores.
All inputs are finite; a program needn't handle non-finite values.
Results may differ from the reference program's by a relative error of at most 0.0051.
Values may be sent and summed in bfloat16 or wider, within the bound.
No kernel may reach another device: no remote copies, remote signals or barrier semaphores. Data moves between devices by JAX's collectives and lax.ppermute only.
A program may use at most 128 MiB of HBM per device.

```python
import jax
import jax.numpy as jnp
from jax import lax

D = 6144
FF = 5376
EXPERTS = 16
BLOCK = 128
TOK_DEV = 384
CAP = 256
TOKENS = 3072
N_DP = 8


def slot_layout(key):
    first_key, second_key, third_key, fourth_key = jax.random.split(key, 4)
    counts = jax.random.randint(first_key, (N_DP,), CAP // 4, CAP + 1)
    fullest = jax.random.randint(second_key, (), 0, N_DP)
    filled = jax.random.randint(fourth_key, (N_DP,), 0, 2) == 1
    counts = jnp.where((jnp.arange(N_DP) == fullest) | filled, CAP, counts)
    orders = jax.vmap(lambda sub_key: jax.random.permutation(sub_key, TOK_DEV))(jax.random.split(third_key, N_DP))[:, :CAP]
    slot_ids = jnp.arange(CAP)
    tokens = jnp.where(slot_ids[None, :] < counts[:, None], orders, TOK_DEV)
    return (counts.astype(jnp.int32), tokens.reshape(-1).astype(jnp.int32))


def draw_row_token(key, part):
    layout = slot_layout(key)
    return layout[1]


def draw_block_count(key, part):
    layout = slot_layout(key)
    return ((layout[0] + BLOCK - 1) // BLOCK).astype(jnp.int32)


def draw_router_logits(key, part):
    key = jax.random.fold_in(key, 7)
    first_key = jax.random.fold_in(key, 0)
    fourth_key = jax.random.fold_in(key, 3)
    expert_ids = jnp.arange(EXPERTS)[None, :]
    leading = jax.random.uniform(fourth_key, (TOKENS, 1), jnp.float32, 2.0, 4.5)
    others = jax.random.normal(first_key, (TOKENS, EXPERTS), jnp.float32)
    return jnp.where(expert_ids == 0, leading, others)


def level_of(rng, shape, pieces, smallest, top_value):
    def one(axis_at, shards_of):
        steps = jax.random.uniform(jax.random.fold_in(jax.random.fold_in(rng, 6), axis_at), (shards_of,), jnp.float32, smallest / len(pieces), top_value / len(pieces))
        return jnp.repeat(jnp.exp(steps), shape[axis_at] // shards_of).reshape((-1,) + (1,) * (len(shape) - axis_at - 1))

    loudness = one(*pieces[0])
    for cut in pieces[1:]:
        loudness = loudness * one(*cut)
    return loudness


def normal_values(key, shape, deviation, bound, shards=(), held_as=jnp.bfloat16):
    loudness = level_of(key, shape, shards, -0.22, 0.18) if shards else 1.0
    array = jax.random.normal(key, shape, jnp.float32) * deviation * loudness
    return jnp.minimum(jnp.maximum(array, -bound), bound).astype(held_as)


def setup_inputs(seed: int = 0) -> dict:
    keys = jax.random.split(jax.random.key(seed), 9)
    pre_gate = normal_values(keys[0], (N_DP * CAP, FF), 1.0, 6.0, ((0, 8), (1, 4)))
    pre_up = normal_values(keys[1], (N_DP * CAP, FF), 1.0, 6.0, ((0, 8), (1, 4)))
    down_weight = normal_values(keys[2], (FF, D), FF ** -0.5, 0.078125, ((0, 4),))
    row_token = draw_row_token(jax.random.fold_in(keys[8], 71), 0)
    block_count = draw_block_count(jax.random.fold_in(keys[8], 71), 0)
    router_logits = draw_router_logits(jax.random.fold_in(keys[8], 71), 0)
    tokens_in = normal_values(keys[6], (TOKENS, D), 1.0, 6.0, ((0, 8), (1, 4)))
    out_grad = normal_values(keys[7], (TOKENS, D), 2.0, 12.0, ((0, 8), (1, 4)))
    return dict(pre_gate=pre_gate, pre_up=pre_up, down_weight=down_weight, row_token=row_token, block_count=block_count, router_logits=router_logits, tokens_in=tokens_in, out_grad=out_grad)


def reference(pre_gate, pre_up, down_weight, row_token, block_count, router_logits, tokens_in, out_grad):
    slot_total = N_DP * CAP
    slot_ids = jnp.arange(slot_total, dtype=jnp.int32)
    device_ids = slot_ids // CAP
    live_slot = ((slot_ids % CAP) // BLOCK < block_count[device_ids]) & (row_token < TOK_DEV)
    global_index = jnp.where(live_slot, device_ids * TOK_DEV + row_token, TOKENS).astype(jnp.int32)
    safe_index = jnp.minimum(global_index, TOKENS - 1)
    router_probs = jax.nn.softmax(router_logits.astype(jnp.float32), axis=-1)
    first_prob = router_probs[:, 0]
    row_prob = jnp.where(live_slot, first_prob[safe_index], 0.0)
    gate_value = pre_gate.astype(jnp.float32)
    up_value = pre_up.astype(jnp.float32)
    sigmoid_gate = jax.nn.sigmoid(gate_value)
    hidden = jnp.where(live_slot[:, None], gate_value * sigmoid_gate * up_value, 0.0).astype(jnp.bfloat16)
    expert_out = jnp.dot(hidden, down_weight, preferred_element_type=jnp.float32)
    combined = jnp.zeros((TOKENS, D), jnp.float32).at[global_index].add(row_prob[:, None] * expert_out, mode="drop").astype(jnp.bfloat16)
    slot_grad = jnp.where(live_slot[:, None], out_grad[safe_index], 0.0).astype(jnp.bfloat16)
    weight_grad = jnp.sum(slot_grad.astype(jnp.float32) * expert_out, axis=1)
    raw_back = lax.dot_general(slot_grad, down_weight, (((1,), (1,)), ((), ())), preferred_element_type=jnp.float32)
    hidden_grad = row_prob[:, None] * raw_back
    grad_up = (hidden_grad * gate_value * sigmoid_gate).astype(jnp.bfloat16)
    grad_gate = (hidden_grad * up_value * sigmoid_gate * (1.0 + gate_value * (1.0 - sigmoid_gate))).astype(jnp.bfloat16)
    token_weight = jnp.zeros((TOKENS,), jnp.float32).at[global_index].add(weight_grad, mode="drop")
    one_hot = (jnp.arange(EXPERTS) == 0).astype(jnp.float32)
    logit_grad = (first_prob[:, None] * (one_hot[None, :] - router_probs) * token_weight[:, None]).astype(jnp.bfloat16)
    router_grad = jnp.dot(logit_grad.T, tokens_in, preferred_element_type=jnp.float32) * (TOKENS ** -0.5)
    return combined, grad_gate, grad_up, router_grad
```

```python
import functools

import jax
import jax.numpy as jnp
from jax import lax
from jax.experimental import pallas as pl
from jax.experimental.pallas import tpu as pltpu
from jax.sharding import PartitionSpec as P

BLOCK = 128
F32 = jnp.float32
BF16 = jnp.bfloat16


def params(mib=24):
    return pltpu.CompilerParams(vmem_limit_bytes=mib * 1024 * 1024)


def cost(flops, size, trans=0):
    return pl.CostEstimate(flops=flops, bytes_accessed=size, transcendentals=trans)


def row_step(rows, most=336):
    best = 16
    for step in range(16, most + 1, 16):
        if rows % step == 0:
            best = step
    return best


def live_lanes(row_ref, count_ref, tok_count):
    rows = row_ref[...]
    slots = lax.broadcasted_iota(jnp.int32, rows.shape, 1)
    return (slots // BLOCK < count_ref[0]) & (rows < tok_count)


def token_of_slot(row_ref, count_ref, tok_count):
    live = live_lanes(row_ref, count_ref, tok_count)
    rows = jnp.where(live, row_ref[...], tok_count)
    tokens = lax.broadcasted_iota(jnp.int32, (tok_count, rows.shape[1]), 0)
    return tokens == rows


def softmax_rows(logits):
    top = jnp.max(logits, axis=0, keepdims=True)
    raised = jnp.exp(logits - top)
    return raised / jnp.sum(raised, axis=0, keepdims=True)


def thirds(value):
    high = value.astype(BF16)
    rest = value - high.astype(F32)
    mid = rest.astype(BF16)
    return high, mid, (rest - mid.astype(F32)).astype(BF16)


def picked(row, mask, dims):
    total = None
    for term in thirds(row):
        part = lax.dot_general(
            jnp.broadcast_to(term, (16, row.shape[1])), mask, (dims, ((), ())), preferred_element_type=F32
        )
        total = part if total is None else total + part
    return total[0:1, :]


def gather_kernel(tok_count, row_ref, grad_ref, *refs):
    n = len(refs) // 2
    outs, made, sem = refs[:n], refs[n:-1], refs[-1]
    rows = row_ref[...]
    column = jnp.broadcast_to(rows, (8, rows.shape[1])).T[:, 0:1]
    tokens = lax.broadcasted_iota(jnp.int32, (rows.shape[1], tok_count), 1)
    mask = (tokens == column).astype(F32).astype(BF16)
    puts = []
    for at, (stage, out) in enumerate(zip(made, outs)):
        width = out.shape[1]
        stage[...] = jnp.dot(
            mask, grad_ref[:, at * width : (at + 1) * width], preferred_element_type=F32
        ).astype(BF16)
        puts.append(pltpu.make_async_copy(stage, out, sem.at[at]))
        puts[-1].start()
    for put in puts:
        put.wait()


def depth_parts(hid):
    half = -(-hid // 512) * 256
    return [(0, half), (half, hid)] if half < hid else [(0, hid)]


def tile_of(ref, rows, me_ref, key, cuts, width):
    flip, cut = key
    at = ((me_ref[0] ^ flip) * cuts + cut) * width
    return ref[rows, pl.ds(pl.multiple_of(at, 128), width)]


def first_forward_kernel(keys, cuts, me_ref, gate_ref, up_ref, weight_ref, *rest):
    n = len(keys)
    outs, kept_ref, hidden_ref, stages = rest[:n], rest[n], rest[n + 1], rest[n + 2 : 2 * n + 2]
    in_sem, out_sem = rest[2 * n + 2 :]
    width = outs[0].shape[1]
    parts = depth_parts(kept_ref.shape[0])

    def fetch(p):
        here = pl.ds(parts[p][0], parts[p][1] - parts[p][0])
        return pltpu.make_async_copy(weight_ref.at[here, :], kept_ref.at[here, :], in_sem.at[p])

    for p in range(len(parts)):
        fetch(p).start()
    gate = gate_ref[...].astype(F32)
    up = up_ref[...].astype(F32)
    hidden_ref[...] = (gate * jax.nn.sigmoid(gate) * up).astype(BF16).T
    puts = []
    for p, (start, stop) in enumerate(parts):
        fetch(p).wait()
        for k, (stage, out) in enumerate(zip(stages, outs)):
            part = jnp.dot(
                hidden_ref[:, start:stop],
                tile_of(kept_ref, pl.ds(start, stop - start), me_ref, keys[k], cuts, width),
                preferred_element_type=F32,
            )
            if p > 0:
                part = part + stage[...].astype(F32)
            stage[...] = part.astype(stage.dtype)
            if p == len(parts) - 1:
                puts.append(pltpu.make_async_copy(stage, out, out_sem.at[k]))
                puts[-1].start()
    for put in puts:
        put.wait()


def next_forward_kernel(keys, cuts, me_ref, row_ref, count_ref, logit_ref, hidden_ref, kept_ref, *refs):
    outs, (prob_ref, pick_ref, weight_ref) = refs[:-3], refs[-3:]
    tok_count = logit_ref.shape[1]
    mask = token_of_slot(row_ref, count_ref, tok_count)
    pick = mask.astype(F32).astype(BF16)
    prob = picked(softmax_rows(logit_ref[...])[0:1, :], pick, ((1,), (0,)))
    prob_ref[...] = prob
    pick_ref[...] = pick
    weight_ref[...] = jnp.sum(jnp.where(mask, prob, 0.0), axis=1, keepdims=True)
    for key, out in zip(keys, outs):
        tile = tile_of(kept_ref, slice(None), me_ref, key, cuts, out.shape[1])
        out[...] = jnp.dot(hidden_ref[...], tile, preferred_element_type=F32).astype(out.dtype)


def times_rows(keys, cuts, me_ref, kept_ref, here, pieces):
    total = None
    for key, piece in zip(keys, pieces):
        part = lax.dot_general(
            tile_of(kept_ref, here, me_ref, key, cuts, piece.shape[1]),
            piece[...],
            (((1,), (1,)), ((), ())),
            preferred_element_type=F32,
        )
        total = part if total is None else total + part
    return total


def dot_kernel(n_pairs, has_dot, *refs):
    total = None
    for k in range(n_pairs):
        product = refs[k][...].astype(F32) * refs[n_pairs + k][...].astype(F32)
        total = product if total is None else total + product
    column = jnp.sum(total, axis=1, keepdims=True)
    row = jnp.broadcast_to(column, (column.shape[0], 128)).T[0:1, :]
    refs[-1][...] = row + refs[-2][...] if has_dot else row


def back_kernel(keys, cuts, has_acc, me_ref, *refs):
    n = len(keys)
    pieces, kept_ref, out_ref = refs[:n], refs[n], refs[-1]
    rows = out_ref.shape[0]
    step = row_step(rows)
    for j in range(rows // step):
        here = pl.ds(j * step, step)
        part = times_rows(keys, cuts, me_ref, kept_ref, here, pieces)
        out_ref[here, :] = part + refs[-2][here, :] if has_acc else part


def final_back_kernel(keys, cuts, me_ref, prob_ref, gate_ref, up_ref, *refs):
    n = len(keys)
    pieces, kept_ref, acc_ref = refs[:n], refs[n], refs[n + 1]
    dgate_ref, dup_ref, dgate, dup, sem = refs[n + 2 :]
    rows = acc_ref.shape[0]
    step = row_step(rows)
    prob = prob_ref[...]
    puts = []
    for j in range(rows // step):
        here = pl.ds(j * step, step)
        raw = acc_ref[here, :] + times_rows(keys, cuts, me_ref, kept_ref, here, pieces)
        gate = gate_ref[here, :].astype(F32)
        up = up_ref[here, :].astype(F32)
        sig = jax.nn.sigmoid(gate)
        act = gate * sig
        scaled = prob * raw
        dup[here, :] = (scaled * act).astype(BF16)
        dgate[here, :] = (scaled * up * sig * (1.0 + gate * (1.0 - sig))).astype(BF16)
        for side, (made, out) in enumerate(((dgate, dgate_ref), (dup, dup_ref))):
            puts.append(pltpu.make_async_copy(made.at[here, :], out.at[here, :], sem.at[side, j]))
            puts[-1].start()
    for put in puts:
        put.wait()


def router_kernel(scale, pick_ref, logit_ref, tokens_ref, *refs):
    dots, out_ref = refs[:-1], refs[-1]
    weight = dots[0][...]
    for other in dots[1:]:
        weight = weight + other[...]
    spread = picked(weight, pick_ref[...], ((1,), (1,)))
    probs = softmax_rows(logit_ref[...])
    expert = lax.broadcasted_iota(jnp.int32, probs.shape, 0)
    hot = jnp.where(expert == 0, 1.0, 0.0)
    logit_grad = (probs[0:1, :] * (hot - probs) * spread).astype(BF16)
    out_ref[...] = jnp.dot(logit_grad, tokens_ref[...], preferred_element_type=F32) * scale


def place_kernel(pick_ref, *refs):
    parts, placed_ref = refs[:-1], refs[-1]
    pick = pick_ref[...]
    value = parts[0][...].astype(F32)
    for part in parts[1:]:
        value = value + part[...].astype(F32)
    high = value.astype(BF16)
    low = (value - high.astype(F32)).astype(BF16)
    placed_ref[...] = jnp.dot(pick, high, preferred_element_type=F32) + jnp.dot(
        pick, low, preferred_element_type=F32
    )


def combine_kernel(cut, n_sums, placed_ref, pick_ref, weight_ref, last_ref, *refs):
    sums, (made, sem) = refs[:n_sums], refs[-2:]
    out_ref = refs[-4] if n_sums else refs[-3]
    rows, width = made.shape
    step = row_step(rows, 128)
    puts = []
    for j in range(rows // step):
        here = pl.ds(j * step, step)
        last = jnp.dot(pick_ref[here, :], last_ref[...], preferred_element_type=F32)
        made[here, :] = (weight_ref[here, :] * (placed_ref[here, :] + last)).astype(BF16)
        puts.append(
            pltpu.make_async_copy(made.at[here, :], out_ref.at[here, pl.ds(cut * width, width)], sem.at[j])
        )
        puts[-1].start()
    if n_sums:
        refs[-3][...] = sums[0][...].astype(F32) + sums[1][...].astype(F32)
    for put in puts:
        put.wait()


def smem():
    return pl.BlockSpec(memory_space=pltpu.SMEM)


def vmem():
    return pl.BlockSpec(memory_space=pltpu.VMEM)


def body(pre_gate, pre_up, down_weight, row_token, block_count, router_logits, tokens_in, out_grad):
    n_et, n_dp = lax.axis_size("et"), lax.axis_size("dp")
    slots, hid = pre_gate.shape
    tok_count, feat = tokens_in.shape
    experts = router_logits.shape[1]
    square = n_et == 4 and feat % 256 == 0
    cuts = 2 if square else 1
    width = feat // cuts
    me = lax.axis_index("et")

    def swap(value, flip, axis="et", size=n_et):
        return lax.ppermute(value, axis, [(i, i ^ flip) for i in range(size)])

    rows = row_token.reshape(1, slots)
    gate_t, up_t, logits_t = pre_gate.T, pre_up.T, router_logits.T

    own = pl.pallas_call(
        functools.partial(gather_kernel, tok_count),
        out_shape=[jax.ShapeDtypeStruct((slots, width), BF16)] * cuts,
        in_specs=[vmem(), vmem()],
        out_specs=[pl.BlockSpec(memory_space=pl.ANY)] * cuts,
        scratch_shapes=[pltpu.VMEM((slots, width), BF16)] * cuts + [pltpu.SemaphoreType.DMA((cuts,))],
        compiler_params=params(60),
        cost_estimate=cost(1, 1),
        name="gather_rows",
    )(rows, out_grad)

    spot, *own = lax.optimization_barrier((me.reshape(1), *own))

    def results(plan):
        kinds = [
            F32 if flip == 0 or (square and (flip, cut) in ((2, 0), (1, 1))) else BF16 for flip, cut in plan
        ]
        return kinds, [jax.ShapeDtypeStruct((slots, width), kind) for kind in kinds]

    if square:
        plans = [[(0, 0), (0, 1), (1, 0), (2, 1)], [(3, 0), (3, 1), (1, 1), (2, 0)]]
    else:
        plans = [[(0, 0)], [(flip, 0) for flip in range(1, n_et)]]
    part = {}
    kinds, shapes = results(plans[0])
    *outs, kept, hidden = pl.pallas_call(
        functools.partial(first_forward_kernel, plans[0], cuts),
        out_shape=shapes
        + [jax.ShapeDtypeStruct(down_weight.shape, BF16), jax.ShapeDtypeStruct((slots, hid), BF16)],
        in_specs=[smem(), vmem(), vmem(), pl.BlockSpec(memory_space=pl.ANY)],
        out_specs=[pl.BlockSpec(memory_space=pl.ANY)] * len(kinds) + [vmem()] * 2,
        scratch_shapes=[pltpu.VMEM((slots, width), kind) for kind in kinds]
        + [pltpu.SemaphoreType.DMA((2,)), pltpu.SemaphoreType.DMA((len(kinds),))],
        compiler_params=params(28),
        cost_estimate=cost(1, 1),
        name="forward_0",
    )(spot, gate_t, up_t, down_weight)
    part.update(zip(plans[0], outs))
    block_count, hidden = lax.optimization_barrier((block_count, hidden))

    if square:
        x0, x1, y1, y0 = swap(own[0], 1), swap(own[1], 1), swap(own[1], 2), swap(own[0], 2)
        x0, y1, hidden = lax.optimization_barrier((x0, y1, hidden))
        far = {(3, 0): swap(x0, 2), (3, 1): swap(y1, 1)}
        near = [{(0, 0): own[0], (0, 1): own[1], (1, 0): x0, (2, 1): y1}, {(1, 1): x1, (2, 0): y0}]
    else:
        far = {(flip, 0): swap(own[0], flip) for flip in range(1, n_et)}
        near = [{(0, 0): own[0]}]
    kinds, shapes = results(plans[1])
    *outs, prob, pick, weight = pl.pallas_call(
        functools.partial(next_forward_kernel, plans[1], cuts),
        out_shape=shapes
        + [
            jax.ShapeDtypeStruct((1, slots), F32),
            jax.ShapeDtypeStruct((tok_count, slots), BF16),
            jax.ShapeDtypeStruct((tok_count, 1), F32),
        ],
        in_specs=[smem(), vmem(), smem()] + [vmem()] * 3,
        out_specs=[vmem()] * (len(kinds) + 3),
        compiler_params=params(),
        cost_estimate=cost(1, 1),
        name="forward_1",
    )(spot, rows, block_count, logits_t, hidden, kept)
    part.update(zip(plans[1], outs))

    acc = None
    for at, pieces in enumerate(near):
        before = [] if acc is None else [acc]
        acc = pl.pallas_call(
            functools.partial(back_kernel, [*pieces], cuts, bool(before)),
            out_shape=jax.ShapeDtypeStruct((hid, slots), F32),
            in_specs=[smem()] + [vmem()] * (len(pieces) + 1 + len(before)),
            out_specs=vmem(),
            compiler_params=params(),
            cost_estimate=cost(1, 1),
            name="back_near_%d" % at,
        )(spot, *pieces.values(), kept, *before)
        if square and at == 0:
            part[3, 0], part[3, 1], acc = lax.optimization_barrier((part[3, 0], part[3, 1], acc))

    dot = None
    for pieces in [*near, far]:
        before = [] if dot is None else [dot]
        if before:
            *values, acc = lax.optimization_barrier((*pieces.values(), acc))
            pieces = dict(zip(pieces, values))
        dot = pl.pallas_call(
            functools.partial(dot_kernel, len(pieces), bool(before)),
            out_shape=jax.ShapeDtypeStruct((1, slots), F32),
            in_specs=[vmem()] * (2 * len(pieces) + len(before)),
            out_specs=vmem(),
            compiler_params=params(),
            cost_estimate=cost(1, 1),
            name="dot_part",
        )(*pieces.values(), *[part[key] for key in pieces], *before)
    dots = [dot] + [swap(dot, flip) for flip in range(1, n_et)]

    step = row_step(hid)
    dgate, dup = pl.pallas_call(
        functools.partial(final_back_kernel, [*far], cuts),
        out_shape=[
            jax.ShapeDtypeStruct((hid, slots), BF16),
            jax.ShapeDtypeStruct((hid, slots), BF16),
        ],
        in_specs=[smem()] + [vmem()] * (len(far) + 5),
        out_specs=[pl.BlockSpec(memory_space=pl.ANY)] * 2,
        scratch_shapes=[
            pltpu.VMEM((hid, slots), BF16),
            pltpu.VMEM((hid, slots), BF16),
            pltpu.SemaphoreType.DMA((2, hid // step)),
        ],
        compiler_params=params(),
        cost_estimate=cost(1, 1),
        name="back_far",
    )(spot, prob, gate_t, up_t, *far.values(), kept, acc)

    if square:
        via_x, via_y = swap(part[3, 0], 1), swap(part[3, 1], 2)
        out_x, out_y, dgate = lax.optimization_barrier((part[1, 0], part[2, 1], dgate))
        *dots, via_x, via_y, dgate = lax.optimization_barrier((*dots, via_x, via_y, dgate))
        direct_x, direct_y = swap(out_x, 1), swap(out_y, 2)
        sum_y = (part[2, 0] + via_x.astype(F32)).astype(BF16)
        sum_x = (part[1, 1] + via_y.astype(F32)).astype(BF16)
        groups = [[part[0, 0], direct_x, swap(sum_y, 2)], [part[0, 1], direct_y, swap(sum_x, 1)]]
    else:
        groups = [[part[0, 0]] + [swap(part[flip, 0], flip) for flip in range(1, n_et)]]

    scale = (tok_count * n_dp) ** -0.5
    router = pl.pallas_call(
        functools.partial(router_kernel, scale),
        out_shape=jax.ShapeDtypeStruct((experts, feat), F32),
        in_specs=[vmem()] * (3 + len(dots)),
        out_specs=vmem(),
        compiler_params=params(),
        cost_estimate=cost(1, 1),
        name="router_part",
    )(pick, logits_t, tokens_in, *dots)
    halves = [router, jnp.zeros_like(router)]
    flip = 1
    while flip < n_dp:
        sent = router if flip == 1 else (halves[0].astype(F32) + halves[1].astype(F32)).astype(BF16)
        if square and flip == 4:
            sent, direct_x, direct_y = lax.optimization_barrier((sent, direct_x, direct_y))
            groups[0][1], groups[1][1] = direct_x, direct_y
        halves = [sent, swap(sent, flip, "dp", n_dp)]
        flip *= 2

    combined = None
    for cut in reversed(range(cuts)):
        *parts, last = groups[cut]
        placed = pl.pallas_call(
            place_kernel,
            out_shape=jax.ShapeDtypeStruct((tok_count, width), F32),
            in_specs=[vmem()] * (1 + len(parts)),
            out_specs=vmem(),
            compiler_params=params(),
            cost_estimate=cost(1, 1),
            name="place_%d" % cut,
        )(pick, *parts)
        before = [] if combined is None else [combined]
        sums = halves if cut == 0 else []
        combined, *router = pl.pallas_call(
            functools.partial(combine_kernel, cut, len(sums)),
            out_shape=[jax.ShapeDtypeStruct((tok_count, feat), BF16)]
            + [jax.ShapeDtypeStruct((experts, feat), F32)] * (len(sums) // 2),
            in_specs=[vmem()] * (4 + len(sums)) + [pl.BlockSpec(memory_space=pl.ANY)] * len(before),
            out_specs=[pl.BlockSpec(memory_space=pl.ANY)] + [vmem()] * (len(sums) // 2),
            scratch_shapes=[
                pltpu.VMEM((tok_count, width), BF16),
                pltpu.SemaphoreType.DMA((tok_count // row_step(tok_count, 128),)),
            ],
            input_output_aliases={4 + len(sums): 0} if before else {},
            compiler_params=params(),
            cost_estimate=cost(1, 1),
            name="combine_%d" % cut,
        )(placed, pick, weight, last, *sums, *before)

    return combined, dgate.T, dup.T, router[0]


def solution(mesh):
    in_specs = (
        P("dp", "et"),
        P("dp", "et"),
        P("et", None),
        P("dp"),
        P("dp"),
        P("dp", None),
        P("dp", "et"),
        P("dp", "et"),
    )
    out_specs = (P("dp", "et"), P("dp", "et"), P("dp", "et"), P(None, "et"))
    return jax.shard_map(body, mesh=mesh, in_specs=in_specs, out_specs=out_specs, check_vma=False)
```

```python
import functools

import jax
import jax.numpy as jnp
from jax import lax
from jax.experimental import pallas as pl
from jax.experimental.pallas import tpu as pltpu
from jax.sharding import PartitionSpec as P

BLOCK = 128
F32 = jnp.float32
BF16 = jnp.bfloat16


def params(mib=24):
    return pltpu.CompilerParams(vmem_limit_bytes=mib * 1024 * 1024)


def cost(flops, size, trans=0):
    return pl.CostEstimate(flops=flops, bytes_accessed=size, transcendentals=trans)


def row_step(rows, most=336):
    best = 16
    for step in range(16, most + 1, 16):
        if rows % step == 0:
            best = step
    return best


def live_lanes(row_ref, count_ref, tok_count):
    rows = row_ref[...]
    slots = lax.broadcasted_iota(jnp.int32, rows.shape, 1)
    return (slots // BLOCK < count_ref[0]) & (rows < tok_count)


def token_of_slot(row_ref, count_ref, tok_count):
    live = live_lanes(row_ref, count_ref, tok_count)
    rows = jnp.where(live, row_ref[...], tok_count)
    tokens = lax.broadcasted_iota(jnp.int32, (tok_count, rows.shape[1]), 0)
    return tokens == rows


def softmax_rows(logits):
    top = jnp.max(logits, axis=0, keepdims=True)
    raised = jnp.exp(logits - top)
    return raised / jnp.sum(raised, axis=0, keepdims=True)


def thirds(value):
    high = value.astype(BF16)
    rest = value - high.astype(F32)
    mid = rest.astype(BF16)
    return high, mid, (rest - mid.astype(F32)).astype(BF16)


def picked(row, mask, dims):
    total = None
    for term in thirds(row):
        part = lax.dot_general(
            jnp.broadcast_to(term, (16, row.shape[1])), mask, (dims, ((), ())), preferred_element_type=F32
        )
        total = part if total is None else total + part
    return total[0:1, :]


def gather_kernel(tok_count, row_hbm, grad_hbm, *refs):
    n = (len(refs) - 3) // 2
    outs, made, (row_ref, grad_ref, sem) = refs[:n], refs[n : 2 * n], refs[2 * n :]
    width = outs[0].shape[1]
    spans = [pl.ds(at * width, width) for at in range(n)]
    fetches = [
        pltpu.make_async_copy(grad_hbm.at[:, span], grad_ref.at[:, span], sem.at[n + at])
        for at, span in enumerate(spans)
    ]
    fetch_rows = pltpu.make_async_copy(row_hbm, row_ref, sem.at[2 * n])
    fetch_rows.start()
    for fetch in fetches:
        fetch.start()
    fetch_rows.wait()
    rows = row_ref[...]
    column = jnp.broadcast_to(rows, (8, rows.shape[1])).T[:, 0:1]
    tokens = lax.broadcasted_iota(jnp.int32, (rows.shape[1], tok_count), 1)
    mask = (tokens == column).astype(F32).astype(BF16)
    puts = []
    for at, (stage, out) in enumerate(zip(made, outs)):
        fetches[at].wait()
        stage[...] = jnp.dot(mask, grad_ref[:, spans[at]], preferred_element_type=F32).astype(BF16)
        puts.append(pltpu.make_async_copy(stage, out, sem.at[at]))
        puts[-1].start()
    for put in puts:
        put.wait()


def depth_parts(hid):
    half = -(-hid // 512) * 256
    return [(0, half), (half, hid)] if half < hid else [(0, hid)]


def tile_of(ref, rows, me_ref, key, cuts, width):
    flip, cut = key
    at = ((me_ref[0] ^ flip) * cuts + cut) * width
    return ref[rows, pl.ds(pl.multiple_of(at, 128), width)]


def first_forward_kernel(keys, cuts, me_ref, gate_ref, up_ref, weight_ref, *rest):
    n = len(keys)
    outs, kept_ref, hidden_ref, stages = rest[:n], rest[n], rest[n + 1], rest[n + 2 : 2 * n + 2]
    in_sem, out_sem = rest[2 * n + 2 :]
    width = outs[0].shape[1]
    parts = depth_parts(kept_ref.shape[0])

    def fetch(p):
        here = pl.ds(parts[p][0], parts[p][1] - parts[p][0])
        return pltpu.make_async_copy(weight_ref.at[here, :], kept_ref.at[here, :], in_sem.at[p])

    for p in range(len(parts)):
        fetch(p).start()
    gate = gate_ref[...].astype(F32)
    up = up_ref[...].astype(F32)
    hidden_ref[...] = (gate * jax.nn.sigmoid(gate) * up).astype(BF16).T
    puts = []
    for p, (start, stop) in enumerate(parts):
        fetch(p).wait()
        for k, (stage, out) in enumerate(zip(stages, outs)):
            part = jnp.dot(
                hidden_ref[:, start:stop],
                tile_of(kept_ref, pl.ds(start, stop - start), me_ref, keys[k], cuts, width),
                preferred_element_type=F32,
            )
            if p > 0:
                part = part + stage[...].astype(F32)
            stage[...] = part.astype(stage.dtype)
            if p == len(parts) - 1:
                puts.append(pltpu.make_async_copy(stage, out, out_sem.at[k]))
                puts[-1].start()
    for put in puts:
        put.wait()


def next_forward_kernel(keys, cuts, me_ref, row_ref, count_ref, logit_ref, hidden_ref, kept_ref, *refs):
    outs, (prob_ref, pick_ref, weight_ref) = refs[:-3], refs[-3:]
    tok_count = logit_ref.shape[1]
    mask = token_of_slot(row_ref, count_ref, tok_count)
    pick = mask.astype(F32).astype(BF16)
    prob = picked(softmax_rows(logit_ref[...])[0:1, :], pick, ((1,), (0,)))
    prob_ref[...] = prob
    pick_ref[...] = pick
    weight_ref[...] = jnp.sum(jnp.where(mask, prob, 0.0), axis=1, keepdims=True)
    for key, out in zip(keys, outs):
        tile = tile_of(kept_ref, slice(None), me_ref, key, cuts, out.shape[1])
        out[...] = jnp.dot(hidden_ref[...], tile, preferred_element_type=F32).astype(out.dtype)


def times_rows(keys, cuts, me_ref, kept_ref, here, pieces):
    total = None
    for key, piece in zip(keys, pieces):
        part = lax.dot_general(
            tile_of(kept_ref, here, me_ref, key, cuts, piece.shape[1]),
            piece[...],
            (((1,), (1,)), ((), ())),
            preferred_element_type=F32,
        )
        total = part if total is None else total + part
    return total


def dot_kernel(n_pairs, has_dot, *refs):
    total = None
    for k in range(n_pairs):
        product = refs[k][...].astype(F32) * refs[n_pairs + k][...].astype(F32)
        total = product if total is None else total + product
    column = jnp.sum(total, axis=1, keepdims=True)
    row = jnp.broadcast_to(column, (column.shape[0], 128)).T[0:1, :]
    refs[-1][...] = row + refs[-2][...] if has_dot else row


def back_kernel(keys, cuts, has_acc, me_ref, *refs):
    n = len(keys)
    pieces, kept_ref, out_ref = refs[:n], refs[n], refs[-1]
    rows = out_ref.shape[0]
    step = row_step(rows)
    for j in range(rows // step):
        here = pl.ds(j * step, step)
        part = times_rows(keys, cuts, me_ref, kept_ref, here, pieces)
        out_ref[here, :] = part + refs[-2][here, :] if has_acc else part


def final_back_kernel(keys, cuts, me_ref, prob_ref, gate_ref, up_ref, *refs):
    n = len(keys)
    pieces, kept_ref, acc_ref = refs[:n], refs[n], refs[n + 1]
    dgate_ref, dup_ref, dgate, dup, sem = refs[n + 2 :]
    rows = acc_ref.shape[0]
    step = row_step(rows)
    prob = prob_ref[...]
    puts = []
    for j in range(rows // step):
        here = pl.ds(j * step, step)
        raw = acc_ref[here, :] + times_rows(keys, cuts, me_ref, kept_ref, here, pieces)
        gate = gate_ref[here, :].astype(F32)
        up = up_ref[here, :].astype(F32)
        sig = jax.nn.sigmoid(gate)
        act = gate * sig
        scaled = prob * raw
        dup[here, :] = (scaled * act).astype(BF16)
        dgate[here, :] = (scaled * up * sig * (1.0 + gate * (1.0 - sig))).astype(BF16)
        for side, (made, out) in enumerate(((dgate, dgate_ref), (dup, dup_ref))):
            puts.append(pltpu.make_async_copy(made.at[here, :], out.at[here, :], sem.at[side, j]))
            puts[-1].start()
    for put in puts:
        put.wait()


def router_kernel(scale, pick_ref, logit_ref, tokens_ref, *refs):
    dots, out_ref = refs[:-1], refs[-1]
    weight = dots[0][...]
    for other in dots[1:]:
        weight = weight + other[...]
    spread = picked(weight, pick_ref[...], ((1,), (1,)))
    probs = softmax_rows(logit_ref[...])
    expert = lax.broadcasted_iota(jnp.int32, probs.shape, 0)
    hot = jnp.where(expert == 0, 1.0, 0.0)
    logit_grad = (probs[0:1, :] * (hot - probs) * spread).astype(BF16)
    out_ref[...] = jnp.dot(logit_grad, tokens_ref[...], preferred_element_type=F32) * scale


def place_kernel(pick_ref, *refs):
    parts, placed_ref = refs[:-1], refs[-1]
    pick = pick_ref[...]
    value = parts[0][...].astype(F32)
    for part in parts[1:]:
        value = value + part[...].astype(F32)
    high = value.astype(BF16)
    low = (value - high.astype(F32)).astype(BF16)
    placed_ref[...] = jnp.dot(pick, high, preferred_element_type=F32) + jnp.dot(
        pick, low, preferred_element_type=F32
    )


def combine_kernel(cut, has_router, placed_ref, pick_ref, weight_ref, last_ref, *refs):
    if has_router:
        *terms, out_ref, router_ref, made, sem, one, two, total, router_sem = refs[:2] + refs[-8:]
        fetches = [
            pltpu.make_async_copy(term, held, router_sem.at[at]) for at, (term, held) in enumerate(zip(terms, (one, two)))
        ]
        for fetch in fetches:
            fetch.start()
    else:
        out_ref, made, sem = refs[-3:]
    rows, width = made.shape
    step = row_step(rows, 128)
    puts = []
    for j in range(rows // step):
        here = pl.ds(j * step, step)
        last = jnp.dot(pick_ref[here, :], last_ref[...], preferred_element_type=F32)
        made[here, :] = (weight_ref[here, :] * (placed_ref[here, :] + last)).astype(BF16)
        puts.append(
            pltpu.make_async_copy(made.at[here, :], out_ref.at[here, pl.ds(cut * width, width)], sem.at[j])
        )
        puts[-1].start()
    if has_router:
        for fetch in fetches:
            fetch.wait()
        total[...] = one[...].astype(F32) + two[...].astype(F32)
        puts.append(pltpu.make_async_copy(total, router_ref, router_sem.at[2]))
        puts[-1].start()
    for put in puts:
        put.wait()


def smem():
    return pl.BlockSpec(memory_space=pltpu.SMEM)


def vmem():
    return pl.BlockSpec(memory_space=pltpu.VMEM)


def body(pre_gate, pre_up, down_weight, row_token, block_count, router_logits, tokens_in, out_grad):
    n_et, n_dp = lax.axis_size("et"), lax.axis_size("dp")
    slots, hid = pre_gate.shape
    tok_count, feat = tokens_in.shape
    experts = router_logits.shape[1]
    square = n_et == 4 and feat % 256 == 0
    cuts = 2 if square else 1
    width = feat // cuts
    me = lax.axis_index("et")

    def swap(value, flip, axis="et", size=n_et):
        return lax.ppermute(value, axis, [(i, i ^ flip) for i in range(size)])

    rows = row_token.reshape(1, slots)
    gate_t, up_t, logits_t = pre_gate.T, pre_up.T, router_logits.T

    own = pl.pallas_call(
        functools.partial(gather_kernel, tok_count),
        out_shape=[jax.ShapeDtypeStruct((slots, width), BF16)] * cuts,
        in_specs=[pl.BlockSpec(memory_space=pl.ANY)] * 2,
        out_specs=[pl.BlockSpec(memory_space=pl.ANY)] * cuts,
        scratch_shapes=[pltpu.VMEM((slots, width), BF16)] * cuts
        + [
            pltpu.VMEM((1, slots), jnp.int32),
            pltpu.VMEM((tok_count, feat), BF16),
            pltpu.SemaphoreType.DMA((2 * cuts + 1,)),
        ],
        compiler_params=params(61),
        cost_estimate=cost(1, 1),
        name="gather_rows",
    )(rows, out_grad)

    spot, *own = lax.optimization_barrier((me.reshape(1), *own))

    def results(plan):
        kinds = [
            F32 if flip == 0 or (square and (flip, cut) in ((2, 0), (1, 1))) else BF16 for flip, cut in plan
        ]
        return kinds, [jax.ShapeDtypeStruct((slots, width), kind) for kind in kinds]

    if square:
        plans = [[(0, 0), (0, 1), (1, 0), (2, 1)], [(3, 0), (3, 1), (1, 1), (2, 0)]]
    else:
        plans = [[(0, 0)], [(flip, 0) for flip in range(1, n_et)]]
    part = {}
    kinds, shapes = results(plans[0])
    *outs, kept, hidden = pl.pallas_call(
        functools.partial(first_forward_kernel, plans[0], cuts),
        out_shape=shapes
        + [jax.ShapeDtypeStruct(down_weight.shape, BF16), jax.ShapeDtypeStruct((slots, hid), BF16)],
        in_specs=[smem(), vmem(), vmem(), pl.BlockSpec(memory_space=pl.ANY)],
        out_specs=[pl.BlockSpec(memory_space=pl.ANY)] * len(kinds) + [vmem()] * 2,
        scratch_shapes=[pltpu.VMEM((slots, width), kind) for kind in kinds]
        + [pltpu.SemaphoreType.DMA((2,)), pltpu.SemaphoreType.DMA((len(kinds),))],
        compiler_params=params(28),
        cost_estimate=cost(1, 1),
        name="forward_0",
    )(spot, gate_t, up_t, down_weight)
    part.update(zip(plans[0], outs))
    block_count, hidden = lax.optimization_barrier((block_count, hidden))

    if square:
        x0, x1, y1, y0 = swap(own[0], 1), swap(own[1], 1), swap(own[1], 2), swap(own[0], 2)
        x0, y1, hidden = lax.optimization_barrier((x0, y1, hidden))
        far = {(3, 0): swap(x0, 2), (3, 1): swap(y1, 1)}
        near = [{(0, 0): own[0], (0, 1): own[1], (1, 0): x0, (2, 1): y1}, {(1, 1): x1, (2, 0): y0}]
    else:
        far = {(flip, 0): swap(own[0], flip) for flip in range(1, n_et)}
        near = [{(0, 0): own[0]}]
    kinds, shapes = results(plans[1])
    *outs, prob, pick, weight = pl.pallas_call(
        functools.partial(next_forward_kernel, plans[1], cuts),
        out_shape=shapes
        + [
            jax.ShapeDtypeStruct((1, slots), F32),
            jax.ShapeDtypeStruct((tok_count, slots), BF16),
            jax.ShapeDtypeStruct((tok_count, 1), F32),
        ],
        in_specs=[smem(), vmem(), smem()] + [vmem()] * 3,
        out_specs=[vmem()] * (len(kinds) + 3),
        compiler_params=params(),
        cost_estimate=cost(1, 1),
        name="forward_1",
    )(spot, rows, block_count, logits_t, hidden, kept)
    part.update(zip(plans[1], outs))

    acc = None
    for at, pieces in enumerate(near):
        before = [] if acc is None else [acc]
        acc = pl.pallas_call(
            functools.partial(back_kernel, [*pieces], cuts, bool(before)),
            out_shape=jax.ShapeDtypeStruct((hid, slots), F32),
            in_specs=[smem()] + [vmem()] * (len(pieces) + 1 + len(before)),
            out_specs=vmem(),
            compiler_params=params(),
            cost_estimate=cost(1, 1),
            name="back_near_%d" % at,
        )(spot, *pieces.values(), kept, *before)
        if square and at == 0:
            part[3, 0], part[3, 1], acc = lax.optimization_barrier((part[3, 0], part[3, 1], acc))

    dot = None
    for pieces in [*near, far]:
        before = [] if dot is None else [dot]
        if before:
            *values, acc = lax.optimization_barrier((*pieces.values(), acc))
            pieces = dict(zip(pieces, values))
        dot = pl.pallas_call(
            functools.partial(dot_kernel, len(pieces), bool(before)),
            out_shape=jax.ShapeDtypeStruct((1, slots), F32),
            in_specs=[vmem()] * (2 * len(pieces) + len(before)),
            out_specs=vmem(),
            compiler_params=params(),
            cost_estimate=cost(1, 1),
            name="dot_part",
        )(*pieces.values(), *[part[key] for key in pieces], *before)
    dots = [dot] + [swap(dot, flip) for flip in range(1, n_et)]

    step = row_step(hid)
    dgate, dup = pl.pallas_call(
        functools.partial(final_back_kernel, [*far], cuts),
        out_shape=[
            jax.ShapeDtypeStruct((hid, slots), BF16),
            jax.ShapeDtypeStruct((hid, slots), BF16),
        ],
        in_specs=[smem()] + [vmem()] * (len(far) + 5),
        out_specs=[pl.BlockSpec(memory_space=pl.ANY)] * 2,
        scratch_shapes=[
            pltpu.VMEM((hid, slots), BF16),
            pltpu.VMEM((hid, slots), BF16),
            pltpu.SemaphoreType.DMA((2, hid // step)),
        ],
        compiler_params=params(),
        cost_estimate=cost(1, 1),
        name="back_far",
    )(spot, prob, gate_t, up_t, *far.values(), kept, acc)

    if square:
        via_x, via_y = swap(part[3, 0], 1), swap(part[3, 1], 2)
        out_x, out_y, dgate = lax.optimization_barrier((part[1, 0], part[2, 1], dgate))
        *dots, via_x, via_y, dgate = lax.optimization_barrier((*dots, via_x, via_y, dgate))
        direct_x, direct_y = swap(out_x, 1), swap(out_y, 2)
        sum_y = (part[2, 0] + via_x.astype(F32)).astype(BF16)
        sum_x = (part[1, 1] + via_y.astype(F32)).astype(BF16)
        groups = [[part[0, 0], direct_x, swap(sum_y, 2)], [part[0, 1], direct_y, swap(sum_x, 1)]]
    else:
        groups = [[part[0, 0]] + [swap(part[flip, 0], flip) for flip in range(1, n_et)]]

    scale = (tok_count * n_dp) ** -0.5
    router = pl.pallas_call(
        functools.partial(router_kernel, scale),
        out_shape=jax.ShapeDtypeStruct((experts, feat), F32),
        in_specs=[vmem()] * (3 + len(dots)),
        out_specs=vmem(),
        compiler_params=params(),
        cost_estimate=cost(1, 1),
        name="router_part",
    )(pick, logits_t, tokens_in, *dots)
    halves = [router, jnp.zeros_like(router)]
    flip = 1
    while flip < n_dp:
        sent = router if flip == 1 else (halves[0].astype(F32) + halves[1].astype(F32)).astype(BF16)
        if square and flip == 4:
            sent, direct_x = lax.optimization_barrier((sent, direct_x))
            groups[0][1] = direct_x
        halves = [sent, swap(sent, flip, "dp", n_dp)]
        flip *= 2

    combined = None
    for cut in reversed(range(cuts)):
        *parts, last = groups[cut]
        placed = pl.pallas_call(
            place_kernel,
            out_shape=jax.ShapeDtypeStruct((tok_count, width), F32),
            in_specs=[vmem()] * (1 + len(parts)),
            out_specs=vmem(),
            compiler_params=params(),
            cost_estimate=cost(1, 1),
            name="place_%d" % cut,
        )(pick, *parts)
        before = [] if combined is None else [combined]
        sums = halves if cut == cuts - 1 else []
        combined, *total = pl.pallas_call(
            functools.partial(combine_kernel, cut, bool(sums)),
            out_shape=[jax.ShapeDtypeStruct((tok_count, feat), BF16)]
            + [jax.ShapeDtypeStruct((experts, feat), F32)] * (len(sums) // 2),
            in_specs=[vmem()] * 4 + [pl.BlockSpec(memory_space=pl.ANY)] * len([*sums, *before]),
            out_specs=[pl.BlockSpec(memory_space=pl.ANY)] * (1 + len(sums) // 2),
            scratch_shapes=[
                pltpu.VMEM((tok_count, width), BF16),
                pltpu.SemaphoreType.DMA((tok_count // row_step(tok_count, 128),)),
            ]
            + [pltpu.VMEM((experts, feat), term.dtype) for term in sums]
            + [pltpu.VMEM((experts, feat), F32), pltpu.SemaphoreType.DMA((3,))] * (len(sums) // 2),
            input_output_aliases={4 + len(sums): 0} if before else {},
            compiler_params=params(),
            cost_estimate=cost(1, 1),
            name="combine_%d" % cut,
        )(placed, pick, weight, last, *sums, *before)
        router = total[0] if total else router

    return combined, dgate.T, dup.T, router


def solution(mesh):
    in_specs = (
        P("dp", "et"),
        P("dp", "et"),
        P("et", None),
        P("dp"),
        P("dp"),
        P("dp", None),
        P("dp", "et"),
        P("dp", "et"),
    )
    out_specs = (P("dp", "et"), P("dp", "et"), P("dp", "et"), P(None, "et"))
    return jax.shard_map(body, mesh=mesh, in_specs=in_specs, out_specs=out_specs, check_vma=False)
```

```python
import functools

import jax
import jax.numpy as jnp
from jax import lax
from jax.experimental import pallas as pl
from jax.experimental.pallas import tpu as pltpu
from jax.sharding import PartitionSpec as P

BLOCK = 128
F32 = jnp.float32
BF16 = jnp.bfloat16


def params(mib=24):
    return pltpu.CompilerParams(vmem_limit_bytes=mib * 1024 * 1024)


def cost(flops, size, trans=0):
    return pl.CostEstimate(flops=flops, bytes_accessed=size, transcendentals=trans)


def row_step(rows, most=336):
    best = 16
    for step in range(16, most + 1, 16):
        if rows % step == 0:
            best = step
    return best


def live_lanes(row_ref, count_ref, tok_count):
    rows = row_ref[...]
    slots = lax.broadcasted_iota(jnp.int32, rows.shape, 1)
    return (slots // BLOCK < count_ref[0]) & (rows < tok_count)


def token_of_slot(row_ref, count_ref, tok_count):
    live = live_lanes(row_ref, count_ref, tok_count)
    rows = jnp.where(live, row_ref[...], tok_count)
    tokens = lax.broadcasted_iota(jnp.int32, (tok_count, rows.shape[1]), 0)
    return tokens == rows


def softmax_rows(logits):
    top = jnp.max(logits, axis=0, keepdims=True)
    raised = jnp.exp(logits - top)
    return raised / jnp.sum(raised, axis=0, keepdims=True)


def thirds(value):
    high = value.astype(BF16)
    rest = value - high.astype(F32)
    mid = rest.astype(BF16)
    return high, mid, (rest - mid.astype(F32)).astype(BF16)


def picked(row, mask, dims):
    total = None
    for term in thirds(row):
        part = lax.dot_general(
            jnp.broadcast_to(term, (16, row.shape[1])), mask, (dims, ((), ())), preferred_element_type=F32
        )
        total = part if total is None else total + part
    return total[0:1, :]


def mask_kernel(row_ref, mask_ref):
    rows = row_ref[...]
    column = jnp.broadcast_to(rows, (8, rows.shape[1])).T[:, 0:1]
    tokens = lax.broadcasted_iota(jnp.int32, mask_ref.shape, 1)
    mask_ref[...] = (tokens == column).astype(F32).astype(BF16)


def gather_kernel(mask_ref, grad_ref, *outs):
    for at, out in enumerate(outs):
        width = out.shape[1]
        out[...] = jnp.dot(
            mask_ref[...], grad_ref[:, at * width : (at + 1) * width], preferred_element_type=F32
        ).astype(BF16)


def depth_parts(hid):
    half = -(-hid // 512) * 256
    return [(0, half), (half, hid)] if half < hid else [(0, hid)]


def tile_of(ref, rows, me_ref, key, cuts, width):
    flip, cut = key
    at = ((me_ref[0] ^ flip) * cuts + cut) * width
    return ref[rows, pl.ds(pl.multiple_of(at, 128), width)]


def first_forward_kernel(keys, cuts, me_ref, gate_ref, up_ref, weight_ref, *rest):
    n = len(keys)
    outs, kept_ref, hidden_ref, stages = rest[:n], rest[n], rest[n + 1], rest[n + 2 : 2 * n + 2]
    in_sem, out_sem = rest[2 * n + 2 :]
    width = outs[0].shape[1]
    parts = depth_parts(kept_ref.shape[0])

    def fetch(p):
        here = pl.ds(parts[p][0], parts[p][1] - parts[p][0])
        return pltpu.make_async_copy(weight_ref.at[here, :], kept_ref.at[here, :], in_sem.at[p])

    for p in range(len(parts)):
        fetch(p).start()
    gate = gate_ref[...].astype(F32)
    up = up_ref[...].astype(F32)
    hidden_ref[...] = (gate * jax.nn.sigmoid(gate) * up).astype(BF16).T
    puts = []
    for p, (start, stop) in enumerate(parts):
        fetch(p).wait()
        for k, (stage, out) in enumerate(zip(stages, outs)):
            part = jnp.dot(
                hidden_ref[:, start:stop],
                tile_of(kept_ref, pl.ds(start, stop - start), me_ref, keys[k], cuts, width),
                preferred_element_type=F32,
            )
            if p > 0:
                part = part + stage[...].astype(F32)
            stage[...] = part.astype(stage.dtype)
            if p == len(parts) - 1:
                puts.append(pltpu.make_async_copy(stage, out, out_sem.at[k]))
                puts[-1].start()
    for put in puts:
        put.wait()


def next_forward_kernel(keys, cuts, me_ref, row_ref, count_ref, logit_ref, hidden_ref, kept_ref, *refs):
    outs, (prob_ref, pick_ref, weight_ref) = refs[:-3], refs[-3:]
    tok_count = logit_ref.shape[1]
    mask = token_of_slot(row_ref, count_ref, tok_count)
    pick = mask.astype(F32).astype(BF16)
    prob = picked(softmax_rows(logit_ref[...])[0:1, :], pick, ((1,), (0,)))
    prob_ref[...] = prob
    pick_ref[...] = pick
    weight_ref[...] = jnp.sum(jnp.where(mask, prob, 0.0), axis=1, keepdims=True)
    for key, out in zip(keys, outs):
        tile = tile_of(kept_ref, slice(None), me_ref, key, cuts, out.shape[1])
        out[...] = jnp.dot(hidden_ref[...], tile, preferred_element_type=F32).astype(out.dtype)


def times_rows(keys, cuts, me_ref, kept_ref, here, pieces):
    total = None
    for key, piece in zip(keys, pieces):
        part = lax.dot_general(
            tile_of(kept_ref, here, me_ref, key, cuts, piece.shape[1]),
            piece[...],
            (((1,), (1,)), ((), ())),
            preferred_element_type=F32,
        )
        total = part if total is None else total + part
    return total


def dot_kernel(n_pairs, has_dot, *refs):
    total = None
    for k in range(n_pairs):
        product = refs[k][...].astype(F32) * refs[n_pairs + k][...].astype(F32)
        total = product if total is None else total + product
    column = jnp.sum(total, axis=1, keepdims=True)
    row = jnp.broadcast_to(column, (column.shape[0], 128)).T[0:1, :]
    refs[-1][...] = row + refs[-2][...] if has_dot else row


def back_kernel(keys, cuts, has_acc, me_ref, *refs):
    n = len(keys)
    pieces, kept_ref, out_ref = refs[:n], refs[n], refs[-1]
    rows = out_ref.shape[0]
    step = row_step(rows)
    for j in range(rows // step):
        here = pl.ds(j * step, step)
        part = times_rows(keys, cuts, me_ref, kept_ref, here, pieces)
        out_ref[here, :] = part + refs[-2][here, :] if has_acc else part


def final_back_kernel(keys, cuts, me_ref, prob_ref, gate_ref, up_ref, *refs):
    n = len(keys)
    pieces, kept_ref, acc_ref = refs[:n], refs[n], refs[n + 1]
    dgate_ref, dup_ref, dgate, dup, sem = refs[n + 2 :]
    rows = acc_ref.shape[0]
    step = row_step(rows)
    prob = prob_ref[...]
    puts = []
    for j in range(rows // step):
        here = pl.ds(j * step, step)
        raw = acc_ref[here, :] + times_rows(keys, cuts, me_ref, kept_ref, here, pieces)
        gate = gate_ref[here, :].astype(F32)
        up = up_ref[here, :].astype(F32)
        sig = jax.nn.sigmoid(gate)
        act = gate * sig
        scaled = prob * raw
        dup[here, :] = (scaled * act).astype(BF16)
        dgate[here, :] = (scaled * up * sig * (1.0 + gate * (1.0 - sig))).astype(BF16)
        for side, (made, out) in enumerate(((dgate, dgate_ref), (dup, dup_ref))):
            puts.append(pltpu.make_async_copy(made.at[here, :], out.at[here, :], sem.at[side, j]))
            puts[-1].start()
    for put in puts:
        put.wait()


def router_kernel(scale, pick_ref, logit_ref, tokens_ref, *refs):
    dots, out_ref = refs[:-1], refs[-1]
    weight = dots[0][...]
    for other in dots[1:]:
        weight = weight + other[...]
    spread = picked(weight, pick_ref[...], ((1,), (1,)))
    probs = softmax_rows(logit_ref[...])
    expert = lax.broadcasted_iota(jnp.int32, probs.shape, 0)
    hot = jnp.where(expert == 0, 1.0, 0.0)
    logit_grad = (probs[0:1, :] * (hot - probs) * spread).astype(BF16)
    out_ref[...] = jnp.dot(logit_grad, tokens_ref[...], preferred_element_type=F32) * scale


def place_kernel(pick_ref, *refs):
    parts, placed_ref = refs[:-1], refs[-1]
    pick = pick_ref[...]
    value = parts[0][...].astype(F32)
    for part in parts[1:]:
        value = value + part[...].astype(F32)
    high = value.astype(BF16)
    low = (value - high.astype(F32)).astype(BF16)
    placed_ref[...] = jnp.dot(pick, high, preferred_element_type=F32) + jnp.dot(
        pick, low, preferred_element_type=F32
    )


def combine_kernel(cut, has_router, placed_ref, pick_ref, weight_ref, last_ref, *refs):
    if has_router:
        *terms, out_ref, router_ref, made, sem, one, two, total, router_sem = refs[:2] + refs[-8:]
        fetches = [
            pltpu.make_async_copy(term, held, router_sem.at[at]) for at, (term, held) in enumerate(zip(terms, (one, two)))
        ]
        for fetch in fetches:
            fetch.start()
    else:
        out_ref, made, sem = refs[-3:]
    rows, width = made.shape
    step = row_step(rows, 128)
    puts = []
    for j in range(rows // step):
        here = pl.ds(j * step, step)
        last = jnp.dot(pick_ref[here, :], last_ref[...], preferred_element_type=F32)
        made[here, :] = (weight_ref[here, :] * (placed_ref[here, :] + last)).astype(BF16)
        puts.append(
            pltpu.make_async_copy(made.at[here, :], out_ref.at[here, pl.ds(cut * width, width)], sem.at[j])
        )
        puts[-1].start()
    if has_router:
        for fetch in fetches:
            fetch.wait()
        total[...] = one[...].astype(F32) + two[...].astype(F32)
        puts.append(pltpu.make_async_copy(total, router_ref, router_sem.at[2]))
        puts[-1].start()
    for put in puts:
        put.wait()


def smem():
    return pl.BlockSpec(memory_space=pltpu.SMEM)


def vmem():
    return pl.BlockSpec(memory_space=pltpu.VMEM)


def body(pre_gate, pre_up, down_weight, row_token, block_count, router_logits, tokens_in, out_grad):
    n_et, n_dp = lax.axis_size("et"), lax.axis_size("dp")
    slots, hid = pre_gate.shape
    tok_count, feat = tokens_in.shape
    experts = router_logits.shape[1]
    square = n_et == 4 and feat % 256 == 0
    cuts = 2 if square else 1
    width = feat // cuts
    me = lax.axis_index("et")

    def swap(value, flip, axis="et", size=n_et):
        return lax.ppermute(value, axis, [(i, i ^ flip) for i in range(size)])

    rows = row_token.reshape(1, slots)
    gate_t, up_t, logits_t = pre_gate.T, pre_up.T, router_logits.T

    places = pl.pallas_call(
        mask_kernel,
        out_shape=jax.ShapeDtypeStruct((slots, tok_count), BF16),
        in_specs=[vmem()],
        out_specs=vmem(),
        compiler_params=params(),
        cost_estimate=cost(10**10, 1),
        name="token_mask",
    )(rows)
    own = pl.pallas_call(
        gather_kernel,
        out_shape=[jax.ShapeDtypeStruct((slots, width), BF16)] * cuts,
        in_specs=[vmem(), vmem()],
        out_specs=[vmem()] * cuts,
        compiler_params=params(),
        cost_estimate=cost(1, 1),
        name="gather_rows",
    )(places, out_grad)

    spot, *own = lax.optimization_barrier((me.reshape(1), *own))

    def results(plan):
        kinds = [
            F32 if flip == 0 or (square and (flip, cut) in ((2, 0), (1, 1))) else BF16 for flip, cut in plan
        ]
        return kinds, [jax.ShapeDtypeStruct((slots, width), kind) for kind in kinds]

    if square:
        plans = [[(0, 0), (0, 1), (1, 0), (2, 1)], [(3, 0), (3, 1), (1, 1), (2, 0)]]
    else:
        plans = [[(0, 0)], [(flip, 0) for flip in range(1, n_et)]]
    part = {}
    kinds, shapes = results(plans[0])
    *outs, kept, hidden = pl.pallas_call(
        functools.partial(first_forward_kernel, plans[0], cuts),
        out_shape=shapes
        + [jax.ShapeDtypeStruct(down_weight.shape, BF16), jax.ShapeDtypeStruct((slots, hid), BF16)],
        in_specs=[smem(), vmem(), vmem(), pl.BlockSpec(memory_space=pl.ANY)],
        out_specs=[pl.BlockSpec(memory_space=pl.ANY)] * len(kinds) + [vmem()] * 2,
        scratch_shapes=[pltpu.VMEM((slots, width), kind) for kind in kinds]
        + [pltpu.SemaphoreType.DMA((2,)), pltpu.SemaphoreType.DMA((len(kinds),))],
        compiler_params=params(28),
        cost_estimate=cost(1, 1),
        name="forward_0",
    )(spot, gate_t, up_t, down_weight)
    part.update(zip(plans[0], outs))
    block_count, hidden = lax.optimization_barrier((block_count, hidden))

    if square:
        x0, x1, y1, y0 = swap(own[0], 1), swap(own[1], 1), swap(own[1], 2), swap(own[0], 2)
        x0, y1, hidden = lax.optimization_barrier((x0, y1, hidden))
        far = {(3, 0): swap(x0, 2), (3, 1): swap(y1, 1)}
        near = [{(0, 0): own[0], (0, 1): own[1], (1, 0): x0, (2, 1): y1}, {(1, 1): x1, (2, 0): y0}]
    else:
        far = {(flip, 0): swap(own[0], flip) for flip in range(1, n_et)}
        near = [{(0, 0): own[0]}]
    kinds, shapes = results(plans[1])
    *outs, prob, pick, weight = pl.pallas_call(
        functools.partial(next_forward_kernel, plans[1], cuts),
        out_shape=shapes
        + [
            jax.ShapeDtypeStruct((1, slots), F32),
            jax.ShapeDtypeStruct((tok_count, slots), BF16),
            jax.ShapeDtypeStruct((tok_count, 1), F32),
        ],
        in_specs=[smem(), vmem(), smem()] + [vmem()] * 3,
        out_specs=[vmem()] * (len(kinds) + 3),
        compiler_params=params(),
        cost_estimate=cost(1, 1),
        name="forward_1",
    )(spot, rows, block_count, logits_t, hidden, kept)
    part.update(zip(plans[1], outs))

    acc = None
    for at, pieces in enumerate(near):
        before = [] if acc is None else [acc]
        acc = pl.pallas_call(
            functools.partial(back_kernel, [*pieces], cuts, bool(before)),
            out_shape=jax.ShapeDtypeStruct((hid, slots), F32),
            in_specs=[smem()] + [vmem()] * (len(pieces) + 1 + len(before)),
            out_specs=vmem(),
            compiler_params=params(),
            cost_estimate=cost(1, 1),
            name="back_near_%d" % at,
        )(spot, *pieces.values(), kept, *before)
        if square and at == 0:
            part[3, 0], part[3, 1], acc = lax.optimization_barrier((part[3, 0], part[3, 1], acc))

    dot = None
    for pieces in [*near, far]:
        before = [] if dot is None else [dot]
        if before:
            *values, acc = lax.optimization_barrier((*pieces.values(), acc))
            pieces = dict(zip(pieces, values))
        dot = pl.pallas_call(
            functools.partial(dot_kernel, len(pieces), bool(before)),
            out_shape=jax.ShapeDtypeStruct((1, slots), F32),
            in_specs=[vmem()] * (2 * len(pieces) + len(before)),
            out_specs=vmem(),
            compiler_params=params(),
            cost_estimate=cost(1, 1),
            name="dot_part",
        )(*pieces.values(), *[part[key] for key in pieces], *before)
    dots = [dot] + [swap(dot, flip) for flip in range(1, n_et)]

    step = row_step(hid)
    dgate, dup = pl.pallas_call(
        functools.partial(final_back_kernel, [*far], cuts),
        out_shape=[
            jax.ShapeDtypeStruct((hid, slots), BF16),
            jax.ShapeDtypeStruct((hid, slots), BF16),
        ],
        in_specs=[smem()] + [vmem()] * (len(far) + 5),
        out_specs=[pl.BlockSpec(memory_space=pl.ANY)] * 2,
        scratch_shapes=[
            pltpu.VMEM((hid, slots), BF16),
            pltpu.VMEM((hid, slots), BF16),
            pltpu.SemaphoreType.DMA((2, hid // step)),
        ],
        compiler_params=params(),
        cost_estimate=cost(1, 1),
        name="back_far",
    )(spot, prob, gate_t, up_t, *far.values(), kept, acc)

    if square:
        via_x, via_y = swap(part[3, 0], 1), swap(part[3, 1], 2)
        out_x, out_y, dgate = lax.optimization_barrier((part[1, 0], part[2, 1], dgate))
        *dots, via_x, via_y, dgate = lax.optimization_barrier((*dots, via_x, via_y, dgate))
        direct_x, direct_y = swap(out_x, 1), swap(out_y, 2)
        sum_y = (part[2, 0] + via_x.astype(F32)).astype(BF16)
        sum_x = (part[1, 1] + via_y.astype(F32)).astype(BF16)
        groups = [[part[0, 0], direct_x, swap(sum_y, 2)], [part[0, 1], direct_y, swap(sum_x, 1)]]
    else:
        groups = [[part[0, 0]] + [swap(part[flip, 0], flip) for flip in range(1, n_et)]]

    scale = (tok_count * n_dp) ** -0.5
    router = pl.pallas_call(
        functools.partial(router_kernel, scale),
        out_shape=jax.ShapeDtypeStruct((experts, feat), F32),
        in_specs=[vmem()] * (3 + len(dots)),
        out_specs=vmem(),
        compiler_params=params(),
        cost_estimate=cost(1, 1),
        name="router_part",
    )(pick, logits_t, tokens_in, *dots)
    halves = [router, jnp.zeros_like(router)]
    flip = 1
    while flip < n_dp:
        sent = router if flip == 1 else (halves[0].astype(F32) + halves[1].astype(F32)).astype(BF16)
        if square and flip == 4:
            sent, direct_x = lax.optimization_barrier((sent, direct_x))
            groups[0][1] = direct_x
        halves = [sent, swap(sent, flip, "dp", n_dp)]
        flip *= 2

    combined = None
    for cut in reversed(range(cuts)):
        *parts, last = groups[cut]
        placed = pl.pallas_call(
            place_kernel,
            out_shape=jax.ShapeDtypeStruct((tok_count, width), F32),
            in_specs=[vmem()] * (1 + len(parts)),
            out_specs=vmem(),
            compiler_params=params(),
            cost_estimate=cost(1, 1),
            name="place_%d" % cut,
        )(pick, *parts)
        before = [] if combined is None else [combined]
        sums = halves if cut == cuts - 1 else []
        combined, *total = pl.pallas_call(
            functools.partial(combine_kernel, cut, bool(sums)),
            out_shape=[jax.ShapeDtypeStruct((tok_count, feat), BF16)]
            + [jax.ShapeDtypeStruct((experts, feat), F32)] * (len(sums) // 2),
            in_specs=[vmem()] * 4 + [pl.BlockSpec(memory_space=pl.ANY)] * len([*sums, *before]),
            out_specs=[pl.BlockSpec(memory_space=pl.ANY)] * (1 + len(sums) // 2),
            scratch_shapes=[
                pltpu.VMEM((tok_count, width), BF16),
                pltpu.SemaphoreType.DMA((tok_count // row_step(tok_count, 128),)),
            ]
            + [pltpu.VMEM((experts, feat), term.dtype) for term in sums]
            + [pltpu.VMEM((experts, feat), F32), pltpu.SemaphoreType.DMA((3,))] * (len(sums) // 2),
            input_output_aliases={4 + len(sums): 0} if before else {},
            compiler_params=params(),
            cost_estimate=cost(1, 1),
            name="combine_%d" % cut,
        )(placed, pick, weight, last, *sums, *before)
        router = total[0] if total else router

    return combined, dgate.T, dup.T, router


def solution(mesh):
    in_specs = (
        P("dp", "et"),
        P("dp", "et"),
        P("et", None),
        P("dp"),
        P("dp"),
        P("dp", None),
        P("dp", "et"),
        P("dp", "et"),
    )
    out_specs = (P("dp", "et"), P("dp", "et"), P("dp", "et"), P(None, "et"))
    return jax.shard_map(body, mesh=mesh, in_specs=in_specs, out_specs=out_specs, check_vma=False)
```

```python
import functools

import jax
import jax.numpy as jnp
from jax import lax
from jax.experimental import pallas as pl
from jax.experimental.pallas import tpu as pltpu
from jax.sharding import PartitionSpec as P

BLOCK = 128
F32 = jnp.float32
BF16 = jnp.bfloat16


def params(mib=24):
    return pltpu.CompilerParams(vmem_limit_bytes=mib * 1024 * 1024)


def cost(flops, size, trans=0):
    return pl.CostEstimate(flops=flops, bytes_accessed=size, transcendentals=trans)


def row_step(rows, most=336):
    best = 16
    for step in range(16, most + 1, 16):
        if rows % step == 0:
            best = step
    return best


def live_lanes(row_ref, count_ref, tok_count):
    rows = row_ref[...]
    slots = lax.broadcasted_iota(jnp.int32, rows.shape, 1)
    return (slots // BLOCK < count_ref[0]) & (rows < tok_count)


def token_of_slot(row_ref, count_ref, tok_count):
    live = live_lanes(row_ref, count_ref, tok_count)
    rows = jnp.where(live, row_ref[...], tok_count)
    tokens = lax.broadcasted_iota(jnp.int32, (tok_count, rows.shape[1]), 0)
    return tokens == rows


def softmax_rows(logits):
    top = jnp.max(logits, axis=0, keepdims=True)
    raised = jnp.exp(logits - top)
    return raised / jnp.sum(raised, axis=0, keepdims=True)


def thirds(value):
    high = value.astype(BF16)
    rest = value - high.astype(F32)
    mid = rest.astype(BF16)
    return high, mid, (rest - mid.astype(F32)).astype(BF16)


def picked(row, mask, dims):
    total = None
    for term in thirds(row):
        part = lax.dot_general(
            jnp.broadcast_to(term, (16, row.shape[1])), mask, (dims, ((), ())), preferred_element_type=F32
        )
        total = part if total is None else total + part
    return total[0:1, :]


def mask_kernel(row_ref, mask_ref):
    rows = row_ref[...]
    column = jnp.broadcast_to(rows, (8, rows.shape[1])).T[:, 0:1]
    tokens = lax.broadcasted_iota(jnp.int32, mask_ref.shape, 1)
    mask_ref[...] = (tokens == column).astype(F32).astype(BF16)


def gather_kernel(mask_ref, grad_ref, *outs):
    for at, out in enumerate(outs):
        width = out.shape[1]
        out[...] = jnp.dot(
            mask_ref[...], grad_ref[:, at * width : (at + 1) * width], preferred_element_type=F32
        ).astype(BF16)


def depth_parts(hid):
    half = -(-hid // 512) * 256
    return [(0, half), (half, hid)] if half < hid else [(0, hid)]


def tile_of(ref, rows, me_ref, key, cuts, width):
    flip, cut = key
    at = ((me_ref[0] ^ flip) * cuts + cut) * width
    return ref[rows, pl.ds(pl.multiple_of(at, 128), width)]


def first_forward_kernel(keys, cuts, me_ref, gate_ref, up_ref, weight_ref, *rest):
    n = len(keys)
    outs, kept_ref, hidden_ref, stages = rest[:n], rest[n], rest[n + 1], rest[n + 2 : 2 * n + 2]
    in_sem, out_sem = rest[2 * n + 2 :]
    width = outs[0].shape[1]
    parts = depth_parts(kept_ref.shape[0])

    def fetch(p):
        here = pl.ds(parts[p][0], parts[p][1] - parts[p][0])
        return pltpu.make_async_copy(weight_ref.at[here, :], kept_ref.at[here, :], in_sem.at[p])

    for p in range(len(parts)):
        fetch(p).start()
    gate = gate_ref[...].astype(F32)
    up = up_ref[...].astype(F32)
    hidden_ref[...] = (gate * jax.nn.sigmoid(gate) * up).astype(BF16).T
    puts = []
    for p, (start, stop) in enumerate(parts):
        fetch(p).wait()
        for k, (stage, out) in enumerate(zip(stages, outs)):
            part = jnp.dot(
                hidden_ref[:, start:stop],
                tile_of(kept_ref, pl.ds(start, stop - start), me_ref, keys[k], cuts, width),
                preferred_element_type=F32,
            )
            if p > 0:
                part = part + stage[...].astype(F32)
            stage[...] = part.astype(stage.dtype)
            if p == len(parts) - 1:
                puts.append(pltpu.make_async_copy(stage, out, out_sem.at[k]))
                puts[-1].start()
    for put in puts:
        put.wait()


def next_forward_kernel(keys, cuts, me_ref, row_ref, count_ref, logit_ref, hidden_ref, kept_ref, *refs):
    outs, (prob_ref, pick_ref, weight_ref) = refs[:-3], refs[-3:]
    tok_count = logit_ref.shape[1]
    mask = token_of_slot(row_ref, count_ref, tok_count)
    pick = mask.astype(F32).astype(BF16)
    prob = picked(softmax_rows(logit_ref[...])[0:1, :], pick, ((1,), (0,)))
    prob_ref[...] = prob
    pick_ref[...] = pick
    weight_ref[...] = jnp.sum(jnp.where(mask, prob, 0.0), axis=1, keepdims=True)
    for key, out in zip(keys, outs):
        tile = tile_of(kept_ref, slice(None), me_ref, key, cuts, out.shape[1])
        out[...] = jnp.dot(hidden_ref[...], tile, preferred_element_type=F32).astype(out.dtype)


def times_rows(keys, cuts, me_ref, kept_ref, here, pieces):
    total = None
    for key, piece in zip(keys, pieces):
        part = lax.dot_general(
            tile_of(kept_ref, here, me_ref, key, cuts, piece.shape[1]),
            piece[...],
            (((1,), (1,)), ((), ())),
            preferred_element_type=F32,
        )
        total = part if total is None else total + part
    return total


def dot_kernel(n_pairs, has_dot, *refs):
    total = None
    for k in range(n_pairs):
        product = refs[k][...].astype(F32) * refs[n_pairs + k][...].astype(F32)
        total = product if total is None else total + product
    column = jnp.sum(total, axis=1, keepdims=True)
    row = jnp.broadcast_to(column, (column.shape[0], 128)).T[0:1, :]
    refs[-1][...] = row + refs[-2][...] if has_dot else row


def back_kernel(keys, cuts, has_acc, me_ref, *refs):
    n = len(keys)
    pieces, kept_ref, out_ref = refs[:n], refs[n], refs[-1]
    rows = out_ref.shape[0]
    step = row_step(rows)
    for j in range(rows // step):
        here = pl.ds(j * step, step)
        part = times_rows(keys, cuts, me_ref, kept_ref, here, pieces)
        out_ref[here, :] = part + refs[-2][here, :] if has_acc else part


def final_back_kernel(keys, cuts, me_ref, prob_ref, gate_ref, up_ref, *refs):
    n = len(keys)
    pieces, kept_ref, acc_ref = refs[:n], refs[n], refs[n + 1]
    dgate_ref, dup_ref, dgate, dup, sem = refs[n + 2 :]
    rows = acc_ref.shape[0]
    step = row_step(rows)
    prob = prob_ref[...]
    puts = []
    for j in range(rows // step):
        here = pl.ds(j * step, step)
        raw = acc_ref[here, :] + times_rows(keys, cuts, me_ref, kept_ref, here, pieces)
        gate = gate_ref[here, :].astype(F32)
        up = up_ref[here, :].astype(F32)
        sig = jax.nn.sigmoid(gate)
        act = gate * sig
        scaled = prob * raw
        dup[here, :] = (scaled * act).astype(BF16)
        dgate[here, :] = (scaled * up * sig * (1.0 + gate * (1.0 - sig))).astype(BF16)
        for side, (made, out) in enumerate(((dgate, dgate_ref), (dup, dup_ref))):
            puts.append(pltpu.make_async_copy(made.at[here, :], out.at[here, :], sem.at[side, j]))
            puts[-1].start()
    for put in puts:
        put.wait()


def router_kernel(scale, pick_ref, logit_ref, tokens_ref, *refs):
    dots, out_ref = refs[:-1], refs[-1]
    weight = dots[0][...]
    for other in dots[1:]:
        weight = weight + other[...]
    spread = picked(weight, pick_ref[...], ((1,), (1,)))
    probs = softmax_rows(logit_ref[...])
    expert = lax.broadcasted_iota(jnp.int32, probs.shape, 0)
    hot = jnp.where(expert == 0, 1.0, 0.0)
    logit_grad = (probs[0:1, :] * (hot - probs) * spread).astype(BF16)
    out_ref[...] = jnp.dot(logit_grad, tokens_ref[...], preferred_element_type=F32) * scale


def place_kernel(has_router, pick_ref, *refs):
    if has_router:
        *parts, one, two, placed_ref, router_ref = refs
        router_ref[...] = one[...].astype(F32) + two[...].astype(F32)
    else:
        *parts, placed_ref = refs
    pick = pick_ref[...]
    value = parts[0][...].astype(F32)
    for part in parts[1:]:
        value = value + part[...].astype(F32)
    high = value.astype(BF16)
    low = (value - high.astype(F32)).astype(BF16)
    placed_ref[...] = jnp.dot(pick, high, preferred_element_type=F32) + jnp.dot(
        pick, low, preferred_element_type=F32
    )


def add_last_kernel(placed_ref, pick_ref, weight_ref, last_ref, out_ref):
    last = jnp.dot(pick_ref[...], last_ref[...], preferred_element_type=F32)
    out_ref[...] = (weight_ref[...] * (placed_ref[...] + last)).astype(BF16)


def combine_kernel(n_done, placed_ref, pick_ref, weight_ref, last_ref, *refs):
    done, (out_ref, made, sem) = refs[:n_done], refs[n_done:]
    rows, width = made.shape
    step = row_step(rows, 128)
    puts = [
        pltpu.make_async_copy(ref, out_ref.at[:, pl.ds((1 + at) * width, width)], sem.at[at])
        for at, ref in enumerate(done)
    ]
    for put in puts:
        put.start()
    for j in range(rows // step):
        here = pl.ds(j * step, step)
        last = jnp.dot(pick_ref[here, :], last_ref[...], preferred_element_type=F32)
        made[here, :] = (weight_ref[here, :] * (placed_ref[here, :] + last)).astype(BF16)
        puts.append(
            pltpu.make_async_copy(made.at[here, :], out_ref.at[here, pl.ds(0, width)], sem.at[n_done + j])
        )
        puts[-1].start()
    for put in puts:
        put.wait()


def smem():
    return pl.BlockSpec(memory_space=pltpu.SMEM)


def vmem():
    return pl.BlockSpec(memory_space=pltpu.VMEM)


def body(pre_gate, pre_up, down_weight, row_token, block_count, router_logits, tokens_in, out_grad):
    n_et, n_dp = lax.axis_size("et"), lax.axis_size("dp")
    slots, hid = pre_gate.shape
    tok_count, feat = tokens_in.shape
    experts = router_logits.shape[1]
    square = n_et == 4 and feat % 256 == 0
    cuts = 2 if square else 1
    width = feat // cuts
    me = lax.axis_index("et")

    def swap(value, flip, axis="et", size=n_et):
        return lax.ppermute(value, axis, [(i, i ^ flip) for i in range(size)])

    rows = row_token.reshape(1, slots)
    gate_t, up_t, logits_t = pre_gate.T, pre_up.T, router_logits.T

    places = pl.pallas_call(
        mask_kernel,
        out_shape=jax.ShapeDtypeStruct((slots, tok_count), BF16),
        in_specs=[vmem()],
        out_specs=vmem(),
        compiler_params=params(),
        cost_estimate=cost(10**10, 1),
        name="token_mask",
    )(rows)
    own = pl.pallas_call(
        gather_kernel,
        out_shape=[jax.ShapeDtypeStruct((slots, width), BF16)] * cuts,
        in_specs=[vmem(), vmem()],
        out_specs=[vmem()] * cuts,
        compiler_params=params(),
        cost_estimate=cost(1, 1),
        name="gather_rows",
    )(places, out_grad)

    spot, *own = lax.optimization_barrier((me.reshape(1), *own))

    def results(plan):
        kinds = [
            F32 if flip == 0 or (square and (flip, cut) in ((2, 0), (1, 1))) else BF16 for flip, cut in plan
        ]
        return kinds, [jax.ShapeDtypeStruct((slots, width), kind) for kind in kinds]

    if square:
        plans = [[(0, 0), (0, 1), (1, 0), (2, 1)], [(3, 0), (3, 1), (1, 1), (2, 0)]]
    else:
        plans = [[(0, 0)], [(flip, 0) for flip in range(1, n_et)]]
    part = {}
    kinds, shapes = results(plans[0])
    *outs, kept, hidden = pl.pallas_call(
        functools.partial(first_forward_kernel, plans[0], cuts),
        out_shape=shapes
        + [jax.ShapeDtypeStruct(down_weight.shape, BF16), jax.ShapeDtypeStruct((slots, hid), BF16)],
        in_specs=[smem(), vmem(), vmem(), pl.BlockSpec(memory_space=pl.ANY)],
        out_specs=[pl.BlockSpec(memory_space=pl.ANY)] * len(kinds) + [vmem()] * 2,
        scratch_shapes=[pltpu.VMEM((slots, width), kind) for kind in kinds]
        + [pltpu.SemaphoreType.DMA((2,)), pltpu.SemaphoreType.DMA((len(kinds),))],
        compiler_params=params(28),
        cost_estimate=cost(1, 1),
        name="forward_0",
    )(spot, gate_t, up_t, down_weight)
    part.update(zip(plans[0], outs))
    block_count, hidden = lax.optimization_barrier((block_count, hidden))

    if square:
        x0, x1, y1, y0 = swap(own[0], 1), swap(own[1], 1), swap(own[1], 2), swap(own[0], 2)
        x0, y1, hidden = lax.optimization_barrier((x0, y1, hidden))
        far = {(3, 0): swap(x0, 2), (3, 1): swap(y1, 1)}
        near = [{(0, 0): own[0], (0, 1): own[1], (1, 0): x0, (2, 1): y1}, {(1, 1): x1, (2, 0): y0}]
    else:
        far = {(flip, 0): swap(own[0], flip) for flip in range(1, n_et)}
        near = [{(0, 0): own[0]}]
    kinds, shapes = results(plans[1])
    *outs, prob, pick, weight = pl.pallas_call(
        functools.partial(next_forward_kernel, plans[1], cuts),
        out_shape=shapes
        + [
            jax.ShapeDtypeStruct((1, slots), F32),
            jax.ShapeDtypeStruct((tok_count, slots), BF16),
            jax.ShapeDtypeStruct((tok_count, 1), F32),
        ],
        in_specs=[smem(), vmem(), smem()] + [vmem()] * 3,
        out_specs=[vmem()] * (len(kinds) + 3),
        compiler_params=params(),
        cost_estimate=cost(1, 1),
        name="forward_1",
    )(spot, rows, block_count, logits_t, hidden, kept)
    part.update(zip(plans[1], outs))

    acc = None
    for at, pieces in enumerate(near):
        before = [] if acc is None else [acc]
        acc = pl.pallas_call(
            functools.partial(back_kernel, [*pieces], cuts, bool(before)),
            out_shape=jax.ShapeDtypeStruct((hid, slots), F32),
            in_specs=[smem()] + [vmem()] * (len(pieces) + 1 + len(before)),
            out_specs=vmem(),
            compiler_params=params(),
            cost_estimate=cost(1, 1),
            name="back_near_%d" % at,
        )(spot, *pieces.values(), kept, *before)
        if square and at == 0:
            part[3, 0], part[3, 1], acc = lax.optimization_barrier((part[3, 0], part[3, 1], acc))

    dot = None
    for pieces in [*near, far]:
        before = [] if dot is None else [dot]
        if before:
            *values, acc = lax.optimization_barrier((*pieces.values(), acc))
            pieces = dict(zip(pieces, values))
        dot = pl.pallas_call(
            functools.partial(dot_kernel, len(pieces), bool(before)),
            out_shape=jax.ShapeDtypeStruct((1, slots), F32),
            in_specs=[vmem()] * (2 * len(pieces) + len(before)),
            out_specs=vmem(),
            compiler_params=params(),
            cost_estimate=cost(1, 1),
            name="dot_part",
        )(*pieces.values(), *[part[key] for key in pieces], *before)
    dots = [dot] + [swap(dot, flip) for flip in range(1, n_et)]

    step = row_step(hid)
    dgate, dup = pl.pallas_call(
        functools.partial(final_back_kernel, [*far], cuts),
        out_shape=[
            jax.ShapeDtypeStruct((hid, slots), BF16),
            jax.ShapeDtypeStruct((hid, slots), BF16),
        ],
        in_specs=[smem()] + [vmem()] * (len(far) + 5),
        out_specs=[pl.BlockSpec(memory_space=pl.ANY)] * 2,
        scratch_shapes=[
            pltpu.VMEM((hid, slots), BF16),
            pltpu.VMEM((hid, slots), BF16),
            pltpu.SemaphoreType.DMA((2, hid // step)),
        ],
        compiler_params=params(),
        cost_estimate=cost(1, 1),
        name="back_far",
    )(spot, prob, gate_t, up_t, *far.values(), kept, acc)

    if square:
        via_x, via_y = swap(part[3, 0], 1), swap(part[3, 1], 2)
        out_x, out_y, dgate = lax.optimization_barrier((part[1, 0], part[2, 1], dgate))
        *dots, via_x, via_y, dgate = lax.optimization_barrier((*dots, via_x, via_y, dgate))
        direct_x, direct_y = swap(out_x, 1), swap(out_y, 2)
        sum_y = (part[2, 0] + via_x.astype(F32)).astype(BF16)
        sum_x = (part[1, 1] + via_y.astype(F32)).astype(BF16)
        groups = [[part[0, 0], direct_x, swap(sum_y, 2)], [part[0, 1], direct_y, swap(sum_x, 1)]]
    else:
        groups = [[part[0, 0]] + [swap(part[flip, 0], flip) for flip in range(1, n_et)]]

    scale = (tok_count * n_dp) ** -0.5
    router = pl.pallas_call(
        functools.partial(router_kernel, scale),
        out_shape=jax.ShapeDtypeStruct((experts, feat), F32),
        in_specs=[vmem()] * (3 + len(dots)),
        out_specs=vmem(),
        compiler_params=params(),
        cost_estimate=cost(1, 1),
        name="router_part",
    )(pick, logits_t, tokens_in, *dots)
    halves = [router, jnp.zeros_like(router)]
    flip = 1
    while flip < n_dp:
        sent = router if flip == 1 else (halves[0].astype(F32) + halves[1].astype(F32)).astype(BF16)
        if square and flip == 4:
            sent, direct_x = lax.optimization_barrier((sent, direct_x))
            groups[0][1] = direct_x
        halves = [sent, swap(sent, flip, "dp", n_dp)]
        flip *= 2

    done = []
    for cut in reversed(range(cuts)):
        *parts, last = groups[cut]
        sums = halves if cut == cuts - 1 else []
        placed, *total = pl.pallas_call(
            functools.partial(place_kernel, bool(sums)),
            out_shape=[jax.ShapeDtypeStruct((tok_count, width), F32)]
            + [jax.ShapeDtypeStruct((experts, feat), F32)] * (len(sums) // 2),
            in_specs=[vmem()] * (1 + len(parts) + len(sums)),
            out_specs=[vmem()] * (1 + len(sums) // 2),
            compiler_params=params(),
            cost_estimate=cost(1, 1),
            name="place_%d" % cut,
        )(pick, *parts, *sums)
        router = total[0] if total else router
        if cut > 0:
            done.append(
                pl.pallas_call(
                    add_last_kernel,
                    out_shape=jax.ShapeDtypeStruct((tok_count, width), BF16),
                    in_specs=[vmem()] * 4,
                    out_specs=vmem(),
                    compiler_params=params(),
                    cost_estimate=cost(1, 1),
                    name="combine_%d" % cut,
                )(placed, pick, weight, last)
            )
    combined = pl.pallas_call(
        functools.partial(combine_kernel, len(done)),
        out_shape=jax.ShapeDtypeStruct((tok_count, feat), BF16),
        in_specs=[vmem()] * (4 + len(done)),
        out_specs=pl.BlockSpec(memory_space=pl.ANY),
        scratch_shapes=[
            pltpu.VMEM((tok_count, width), BF16),
            pltpu.SemaphoreType.DMA((len(done) + tok_count // row_step(tok_count, 128),)),
        ],
        compiler_params=params(),
        cost_estimate=cost(1, 1),
        name="combine_0",
    )(placed, pick, weight, last, *done)

    return combined, dgate.T, dup.T, router


def solution(mesh):
    in_specs = (
        P("dp", "et"),
        P("dp", "et"),
        P("et", None),
        P("dp"),
        P("dp"),
        P("dp", None),
        P("dp", "et"),
        P("dp", "et"),
    )
    out_specs = (P("dp", "et"), P("dp", "et"), P("dp", "et"), P(None, "et"))
    return jax.shard_map(body, mesh=mesh, in_specs=in_specs, out_specs=out_specs, check_vma=False)
```

```python
import functools

import jax
import jax.numpy as jnp
from jax import lax
from jax.experimental import pallas as pl
from jax.experimental.pallas import tpu as pltpu
from jax.sharding import PartitionSpec as P

BLOCK = 128
F32 = jnp.float32
BF16 = jnp.bfloat16


def params(mib=24):
    return pltpu.CompilerParams(vmem_limit_bytes=mib * 1024 * 1024)


def cost(flops, size, trans=0):
    return pl.CostEstimate(flops=flops, bytes_accessed=size, transcendentals=trans)


def row_step(rows, most=336):
    best = 16
    for step in range(16, most + 1, 16):
        if rows % step == 0:
            best = step
    return best


def live_lanes(row_ref, count_ref, tok_count):
    rows = row_ref[...]
    slots = lax.broadcasted_iota(jnp.int32, rows.shape, 1)
    return (slots // BLOCK < count_ref[0]) & (rows < tok_count)


def token_of_slot(row_ref, count_ref, tok_count):
    live = live_lanes(row_ref, count_ref, tok_count)
    rows = jnp.where(live, row_ref[...], tok_count)
    tokens = lax.broadcasted_iota(jnp.int32, (tok_count, rows.shape[1]), 0)
    return tokens == rows


def softmax_rows(logits):
    top = jnp.max(logits, axis=0, keepdims=True)
    raised = jnp.exp(logits - top)
    return raised / jnp.sum(raised, axis=0, keepdims=True)


def thirds(value):
    high = value.astype(BF16)
    rest = value - high.astype(F32)
    mid = rest.astype(BF16)
    return high, mid, (rest - mid.astype(F32)).astype(BF16)


def picked(row, mask, dims):
    total = None
    for term in thirds(row):
        part = lax.dot_general(
            jnp.broadcast_to(term, (16, row.shape[1])), mask, (dims, ((), ())), preferred_element_type=F32
        )
        total = part if total is None else total + part
    return total[0:1, :]


def token_kernel(ids_ref):
    ids_ref[...] = lax.broadcasted_iota(jnp.int32, ids_ref.shape, 1)


def mask_kernel(ids_ref, row_ref, mask_ref):
    rows = row_ref[...]
    column = jnp.broadcast_to(rows, (8, rows.shape[1])).T[:, 0:1]
    mask_ref[...] = (ids_ref[0:1, :] == column).astype(F32).astype(BF16)


def gather_kernel(mask_ref, grad_ref, *outs):
    for at, out in enumerate(outs):
        width = out.shape[1]
        out[...] = jnp.dot(
            mask_ref[...], grad_ref[:, at * width : (at + 1) * width], preferred_element_type=F32
        ).astype(BF16)


def depth_parts(hid):
    half = -(-hid // 512) * 256
    return [(0, half), (half, hid)] if half < hid else [(0, hid)]


def tile_of(ref, rows, me_ref, key, cuts, width):
    flip, cut = key
    at = ((me_ref[0] ^ flip) * cuts + cut) * width
    return ref[rows, pl.ds(pl.multiple_of(at, 128), width)]


def first_forward_kernel(keys, cuts, me_ref, gate_ref, up_ref, weight_ref, *rest):
    n = len(keys)
    outs, kept_ref, hidden_ref, stages = rest[:n], rest[n], rest[n + 1], rest[n + 2 : 2 * n + 2]
    in_sem, out_sem = rest[2 * n + 2 :]
    width = outs[0].shape[1]
    parts = depth_parts(kept_ref.shape[0])

    def fetch(p):
        here = pl.ds(parts[p][0], parts[p][1] - parts[p][0])
        return pltpu.make_async_copy(weight_ref.at[here, :], kept_ref.at[here, :], in_sem.at[p])

    for p in range(len(parts)):
        fetch(p).start()
    gate = gate_ref[...].astype(F32)
    up = up_ref[...].astype(F32)
    hidden_ref[...] = (gate * jax.nn.sigmoid(gate) * up).astype(BF16).T
    puts = []
    for p, (start, stop) in enumerate(parts):
        fetch(p).wait()
        for k, (stage, out) in enumerate(zip(stages, outs)):
            part = jnp.dot(
                hidden_ref[:, start:stop],
                tile_of(kept_ref, pl.ds(start, stop - start), me_ref, keys[k], cuts, width),
                preferred_element_type=F32,
            )
            if p > 0:
                part = part + stage[...].astype(F32)
            stage[...] = part.astype(stage.dtype)
            if p == len(parts) - 1:
                puts.append(pltpu.make_async_copy(stage, out, out_sem.at[k]))
                puts[-1].start()
    for put in puts:
        put.wait()


def next_forward_kernel(keys, cuts, me_ref, row_ref, count_ref, logit_ref, hidden_ref, kept_ref, *refs):
    outs, (prob_ref, pick_ref, weight_ref) = refs[:-3], refs[-3:]
    tok_count = logit_ref.shape[1]
    mask = token_of_slot(row_ref, count_ref, tok_count)
    pick = mask.astype(F32).astype(BF16)
    prob = picked(softmax_rows(logit_ref[...])[0:1, :], pick, ((1,), (0,)))
    prob_ref[...] = prob
    pick_ref[...] = pick
    weight_ref[...] = jnp.sum(jnp.where(mask, prob, 0.0), axis=1, keepdims=True)
    for key, out in zip(keys, outs):
        tile = tile_of(kept_ref, slice(None), me_ref, key, cuts, out.shape[1])
        out[...] = jnp.dot(hidden_ref[...], tile, preferred_element_type=F32).astype(out.dtype)


def times_rows(keys, cuts, me_ref, kept_ref, here, pieces):
    total = None
    for key, piece in zip(keys, pieces):
        part = lax.dot_general(
            tile_of(kept_ref, here, me_ref, key, cuts, piece.shape[1]),
            piece[...],
            (((1,), (1,)), ((), ())),
            preferred_element_type=F32,
        )
        total = part if total is None else total + part
    return total


def dot_kernel(n_pairs, has_dot, *refs):
    total = None
    for k in range(n_pairs):
        product = refs[k][...].astype(F32) * refs[n_pairs + k][...].astype(F32)
        total = product if total is None else total + product
    column = jnp.sum(total, axis=1, keepdims=True)
    row = jnp.broadcast_to(column, (column.shape[0], 128)).T[0:1, :]
    refs[-1][...] = row + refs[-2][...] if has_dot else row


def back_kernel(keys, cuts, has_acc, me_ref, *refs):
    n = len(keys)
    pieces, kept_ref, out_ref = refs[:n], refs[n], refs[-1]
    rows = out_ref.shape[0]
    step = row_step(rows)
    for j in range(rows // step):
        here = pl.ds(j * step, step)
        part = times_rows(keys, cuts, me_ref, kept_ref, here, pieces)
        out_ref[here, :] = part + refs[-2][here, :] if has_acc else part


def final_back_kernel(keys, cuts, me_ref, prob_ref, gate_ref, up_ref, *refs):
    n = len(keys)
    pieces, kept_ref, acc_ref = refs[:n], refs[n], refs[n + 1]
    dgate_ref, dup_ref, dgate, dup, sem = refs[n + 2 :]
    rows = acc_ref.shape[0]
    step = row_step(rows)
    prob = prob_ref[...]
    puts = []
    for j in range(rows // step):
        here = pl.ds(j * step, step)
        raw = acc_ref[here, :] + times_rows(keys, cuts, me_ref, kept_ref, here, pieces)
        gate = gate_ref[here, :].astype(F32)
        up = up_ref[here, :].astype(F32)
        sig = jax.nn.sigmoid(gate)
        act = gate * sig
        scaled = prob * raw
        dup[here, :] = (scaled * act).astype(BF16)
        dgate[here, :] = (scaled * up * sig * (1.0 + gate * (1.0 - sig))).astype(BF16)
        for side, (made, out) in enumerate(((dgate, dgate_ref), (dup, dup_ref))):
            puts.append(pltpu.make_async_copy(made.at[here, :], out.at[here, :], sem.at[side, j]))
            puts[-1].start()
    for put in puts:
        put.wait()


def router_kernel(scale, pick_ref, logit_ref, tokens_ref, *refs):
    dots, out_ref = refs[:-1], refs[-1]
    weight = dots[0][...]
    for other in dots[1:]:
        weight = weight + other[...]
    spread = picked(weight, pick_ref[...], ((1,), (1,)))
    probs = softmax_rows(logit_ref[...])
    expert = lax.broadcasted_iota(jnp.int32, probs.shape, 0)
    hot = jnp.where(expert == 0, 1.0, 0.0)
    logit_grad = (probs[0:1, :] * (hot - probs) * spread).astype(BF16)
    out_ref[...] = jnp.dot(logit_grad, tokens_ref[...], preferred_element_type=F32) * scale


def place_kernel(has_router, pick_ref, *refs):
    if has_router:
        *parts, one, two, placed_ref, router_ref = refs
        router_ref[...] = one[...].astype(F32) + two[...].astype(F32)
    else:
        *parts, placed_ref = refs
    pick = pick_ref[...]
    value = parts[0][...].astype(F32)
    for part in parts[1:]:
        value = value + part[...].astype(F32)
    high = value.astype(BF16)
    low = (value - high.astype(F32)).astype(BF16)
    placed_ref[...] = jnp.dot(pick, high, preferred_element_type=F32) + jnp.dot(
        pick, low, preferred_element_type=F32
    )


def add_last_kernel(placed_ref, pick_ref, weight_ref, last_ref, out_ref):
    last = jnp.dot(pick_ref[...], last_ref[...], preferred_element_type=F32)
    out_ref[...] = (weight_ref[...] * (placed_ref[...] + last)).astype(BF16)


def combine_kernel(n_done, placed_ref, pick_ref, weight_ref, last_ref, *refs):
    done, (out_ref, made, sem) = refs[:n_done], refs[n_done:]
    rows, width = made.shape
    step = row_step(rows, 128)
    puts = [
        pltpu.make_async_copy(ref, out_ref.at[:, pl.ds((1 + at) * width, width)], sem.at[at])
        for at, ref in enumerate(done)
    ]
    for put in puts:
        put.start()
    for j in range(rows // step):
        here = pl.ds(j * step, step)
        last = jnp.dot(pick_ref[here, :], last_ref[...], preferred_element_type=F32)
        made[here, :] = (weight_ref[here, :] * (placed_ref[here, :] + last)).astype(BF16)
        puts.append(
            pltpu.make_async_copy(made.at[here, :], out_ref.at[here, pl.ds(0, width)], sem.at[n_done + j])
        )
        puts[-1].start()
    for put in puts:
        put.wait()


def smem():
    return pl.BlockSpec(memory_space=pltpu.SMEM)


def vmem():
    return pl.BlockSpec(memory_space=pltpu.VMEM)


def body(pre_gate, pre_up, down_weight, row_token, block_count, router_logits, tokens_in, out_grad):
    n_et, n_dp = lax.axis_size("et"), lax.axis_size("dp")
    slots, hid = pre_gate.shape
    tok_count, feat = tokens_in.shape
    experts = router_logits.shape[1]
    square = n_et == 4 and feat % 256 == 0
    cuts = 2 if square else 1
    width = feat // cuts
    me = lax.axis_index("et")

    def swap(value, flip, axis="et", size=n_et):
        return lax.ppermute(value, axis, [(i, i ^ flip) for i in range(size)])

    rows = row_token.reshape(1, slots)
    gate_t, up_t, logits_t = pre_gate.T, pre_up.T, router_logits.T

    ids = pl.pallas_call(
        token_kernel,
        out_shape=jax.ShapeDtypeStruct((8, tok_count), jnp.int32),
        out_specs=vmem(),
        compiler_params=params(),
        cost_estimate=cost(10**10, 1),
        name="token_ids",
    )()
    places = pl.pallas_call(
        mask_kernel,
        out_shape=jax.ShapeDtypeStruct((slots, tok_count), BF16),
        in_specs=[vmem()] * 2,
        out_specs=vmem(),
        compiler_params=params(),
        cost_estimate=cost(1, 1),
        name="token_mask",
    )(ids, rows)
    own = pl.pallas_call(
        gather_kernel,
        out_shape=[jax.ShapeDtypeStruct((slots, width), BF16)] * cuts,
        in_specs=[vmem(), vmem()],
        out_specs=[vmem()] * cuts,
        compiler_params=params(),
        cost_estimate=cost(1, 1),
        name="gather_rows",
    )(places, out_grad)

    spot, *own = lax.optimization_barrier((me.reshape(1), *own))

    def results(plan):
        kinds = [
            F32 if flip == 0 or (square and (flip, cut) in ((2, 0), (1, 1))) else BF16 for flip, cut in plan
        ]
        return kinds, [jax.ShapeDtypeStruct((slots, width), kind) for kind in kinds]

    if square:
        plans = [[(0, 0), (0, 1), (1, 0), (2, 1)], [(3, 0), (3, 1), (1, 1), (2, 0)]]
    else:
        plans = [[(0, 0)], [(flip, 0) for flip in range(1, n_et)]]
    part = {}
    kinds, shapes = results(plans[0])
    *outs, kept, hidden = pl.pallas_call(
        functools.partial(first_forward_kernel, plans[0], cuts),
        out_shape=shapes
        + [jax.ShapeDtypeStruct(down_weight.shape, BF16), jax.ShapeDtypeStruct((slots, hid), BF16)],
        in_specs=[smem(), vmem(), vmem(), pl.BlockSpec(memory_space=pl.ANY)],
        out_specs=[pl.BlockSpec(memory_space=pl.ANY)] * len(kinds) + [vmem()] * 2,
        scratch_shapes=[pltpu.VMEM((slots, width), kind) for kind in kinds]
        + [pltpu.SemaphoreType.DMA((2,)), pltpu.SemaphoreType.DMA((len(kinds),))],
        compiler_params=params(28),
        cost_estimate=cost(1, 1),
        name="forward_0",
    )(spot, gate_t, up_t, down_weight)
    part.update(zip(plans[0], outs))
    block_count, hidden = lax.optimization_barrier((block_count, hidden))

    if square:
        x0, x1, y1, y0 = swap(own[0], 1), swap(own[1], 1), swap(own[1], 2), swap(own[0], 2)
        x0, y1, hidden = lax.optimization_barrier((x0, y1, hidden))
        far = {(3, 0): swap(x0, 2), (3, 1): swap(y1, 1)}
        near = [{(0, 0): own[0], (0, 1): own[1], (1, 0): x0, (2, 1): y1}, {(1, 1): x1, (2, 0): y0}]
    else:
        far = {(flip, 0): swap(own[0], flip) for flip in range(1, n_et)}
        near = [{(0, 0): own[0]}]
    kinds, shapes = results(plans[1])
    *outs, prob, pick, weight = pl.pallas_call(
        functools.partial(next_forward_kernel, plans[1], cuts),
        out_shape=shapes
        + [
            jax.ShapeDtypeStruct((1, slots), F32),
            jax.ShapeDtypeStruct((tok_count, slots), BF16),
            jax.ShapeDtypeStruct((tok_count, 1), F32),
        ],
        in_specs=[smem(), vmem(), smem()] + [vmem()] * 3,
        out_specs=[vmem()] * (len(kinds) + 3),
        compiler_params=params(),
        cost_estimate=cost(1, 1),
        name="forward_1",
    )(spot, rows, block_count, logits_t, hidden, kept)
    part.update(zip(plans[1], outs))

    acc = None
    for at, pieces in enumerate(near):
        before = [] if acc is None else [acc]
        acc = pl.pallas_call(
            functools.partial(back_kernel, [*pieces], cuts, bool(before)),
            out_shape=jax.ShapeDtypeStruct((hid, slots), F32),
            in_specs=[smem()] + [vmem()] * (len(pieces) + 1 + len(before)),
            out_specs=vmem(),
            compiler_params=params(),
            cost_estimate=cost(1, 1),
            name="back_near_%d" % at,
        )(spot, *pieces.values(), kept, *before)
        if square and at == 0:
            part[3, 0], part[3, 1], acc = lax.optimization_barrier((part[3, 0], part[3, 1], acc))

    dot = None
    for pieces in [*near, far]:
        before = [] if dot is None else [dot]
        if before:
            *values, acc = lax.optimization_barrier((*pieces.values(), acc))
            pieces = dict(zip(pieces, values))
        dot = pl.pallas_call(
            functools.partial(dot_kernel, len(pieces), bool(before)),
            out_shape=jax.ShapeDtypeStruct((1, slots), F32),
            in_specs=[vmem()] * (2 * len(pieces) + len(before)),
            out_specs=vmem(),
            compiler_params=params(),
            cost_estimate=cost(1, 1),
            name="dot_part",
        )(*pieces.values(), *[part[key] for key in pieces], *before)
    dots = [dot] + [swap(dot, flip) for flip in range(1, n_et)]

    step = row_step(hid)
    dgate, dup = pl.pallas_call(
        functools.partial(final_back_kernel, [*far], cuts),
        out_shape=[
            jax.ShapeDtypeStruct((hid, slots), BF16),
            jax.ShapeDtypeStruct((hid, slots), BF16),
        ],
        in_specs=[smem()] + [vmem()] * (len(far) + 5),
        out_specs=[pl.BlockSpec(memory_space=pl.ANY)] * 2,
        scratch_shapes=[
            pltpu.VMEM((hid, slots), BF16),
            pltpu.VMEM((hid, slots), BF16),
            pltpu.SemaphoreType.DMA((2, hid // step)),
        ],
        compiler_params=params(),
        cost_estimate=cost(1, 1),
        name="back_far",
    )(spot, prob, gate_t, up_t, *far.values(), kept, acc)

    if square:
        via_x, via_y = swap(part[3, 0], 1), swap(part[3, 1], 2)
        out_x, out_y, dgate = lax.optimization_barrier((part[1, 0], part[2, 1], dgate))
        out_x, via_y = lax.optimization_barrier((out_x, via_y))
        *dots, via_x, via_y, dgate = lax.optimization_barrier((*dots, via_x, via_y, dgate))
        direct_x, direct_y = swap(out_x, 1), swap(out_y, 2)
        sum_y = (part[2, 0] + via_x.astype(F32)).astype(BF16)
        sum_x = (part[1, 1] + via_y.astype(F32)).astype(BF16)
        groups = [[part[0, 0], direct_x, swap(sum_y, 2)], [part[0, 1], direct_y, swap(sum_x, 1)]]
    else:
        groups = [[part[0, 0]] + [swap(part[flip, 0], flip) for flip in range(1, n_et)]]

    scale = (tok_count * n_dp) ** -0.5
    router = pl.pallas_call(
        functools.partial(router_kernel, scale),
        out_shape=jax.ShapeDtypeStruct((experts, feat), F32),
        in_specs=[vmem()] * (3 + len(dots)),
        out_specs=vmem(),
        compiler_params=params(),
        cost_estimate=cost(1, 1),
        name="router_part",
    )(pick, logits_t, tokens_in, *dots)
    halves = [router, jnp.zeros_like(router)]
    flip = 1
    while flip < n_dp:
        sent = router if flip == 1 else (halves[0].astype(F32) + halves[1].astype(F32)).astype(BF16)
        if square and flip == 4:
            sent, direct_x = lax.optimization_barrier((sent, direct_x))
            groups[0][1] = direct_x
        halves = [sent, swap(sent, flip, "dp", n_dp)]
        flip *= 2

    done = []
    for cut in reversed(range(cuts)):
        *parts, last = groups[cut]
        sums = halves if cut == cuts - 1 else []
        placed, *total = pl.pallas_call(
            functools.partial(place_kernel, bool(sums)),
            out_shape=[jax.ShapeDtypeStruct((tok_count, width), F32)]
            + [jax.ShapeDtypeStruct((experts, feat), F32)] * (len(sums) // 2),
            in_specs=[vmem()] * (1 + len(parts) + len(sums)),
            out_specs=[vmem()] * (1 + len(sums) // 2),
            compiler_params=params(),
            cost_estimate=cost(1, 1),
            name="place_%d" % cut,
        )(pick, *parts, *sums)
        router = total[0] if total else router
        if cut > 0:
            done.append(
                pl.pallas_call(
                    add_last_kernel,
                    out_shape=jax.ShapeDtypeStruct((tok_count, width), BF16),
                    in_specs=[vmem()] * 4,
                    out_specs=vmem(),
                    compiler_params=params(),
                    cost_estimate=cost(1, 1),
                    name="combine_%d" % cut,
                )(placed, pick, weight, last)
            )
    combined = pl.pallas_call(
        functools.partial(combine_kernel, len(done)),
        out_shape=jax.ShapeDtypeStruct((tok_count, feat), BF16),
        in_specs=[vmem()] * (4 + len(done)),
        out_specs=pl.BlockSpec(memory_space=pl.ANY),
        scratch_shapes=[
            pltpu.VMEM((tok_count, width), BF16),
            pltpu.SemaphoreType.DMA((len(done) + tok_count // row_step(tok_count, 128),)),
        ],
        compiler_params=params(),
        cost_estimate=cost(1, 1),
        name="combine_0",
    )(placed, pick, weight, last, *done)

    return combined, dgate.T, dup.T, router


def solution(mesh):
    in_specs = (
        P("dp", "et"),
        P("dp", "et"),
        P("et", None),
        P("dp"),
        P("dp"),
        P("dp", None),
        P("dp", "et"),
        P("dp", "et"),
    )
    out_specs = (P("dp", "et"), P("dp", "et"), P("dp", "et"), P(None, "et"))
    return jax.shard_map(body, mesh=mesh, in_specs=in_specs, out_specs=out_specs, check_vma=False)
```
